256 devices in a mesh: section: 16 (over y_hi, z), blk: 16 (over y_lo, x, core).
Axes of the slice: x: 4, y: 4 (y_hi: 2, y_lo: 2; y = y_hi * 2 + y_lo), z: 8, core: 2. Of those that a mesh axis runs over, the one named last changes fastest.
Arguments:
- waiting: bfloat16 [16, 512, 3072], P('section', 'blk'), may hold values from -12 to 12
- entering: bfloat16 [3, 512, 3072], P(None, 'blk'), may hold values from -12 to 12
- patch_order: int32 [12], replicated, may hold values from 0 to 11, each once
- step_index: int32 [1], replicated, may hold values from 0 to 27
- modulation: float32 [16, 28, 3, 3072], P('section'), may hold values from -4 to 4
- projection: bfloat16 [16, 3072, 3, 2048], P('section', None, None, 'blk'), may hold values from -0.109375 to 0.109375
- key_gain: float32 [16, 2048], P('section', 'blk'), may hold values from 2 to 3
- output_weight: bfloat16 [16, 2048, 3072], P('section', 'blk'), may hold values from -0.125 to 0.125
- stale_keys: bfloat16 [16, 12, 512, 2048], P('section', None, None, 'blk'), may hold values from -4 to 4
- stale_values: bfloat16 [16, 12, 512, 2048], P('section', None, None, 'blk'), may hold values from -4 to 4
Outputs:
- layer_out: bfloat16 [16, 4, 512, 3072], P('section', None, 'blk')
- fresh_kv: bfloat16 [16, 4, 512, 2, 2048], P('section', None, None, None, 'blk')
The draws below stay inside these ranges and needn't reach their ends.
All inputs are finite; a program needn't handle non-finite values.
Results may differ from the reference program's by a relative error of at most 0.015.
Values may be sent and summed in bfloat16 or wider, within the bound.
No kernel may reach another device: no remote copies, remote signals or barrier semaphores. Data moves between devices by JAX's collectives and lax.ppermute only.
A program may use at most 128 MiB of HBM per device.

```python
import math
import jax
import jax.numpy as jnp
from jax import lax

D = 3072
HEADS = 16
HD = 128
PATCHES = 12
TICKS = 4
STEPS = 28
TOKP = 512
N_SECTION = 16
N_BLK = 16


def spread_rows(seed_key, shape):
    base_key, row_key, column_key = jax.random.split(seed_key, 3)
    column_scale = jnp.exp(jax.random.uniform(column_key, (shape[-1],), jnp.float32, -1.15, 1.15))
    row_scale = jnp.exp(jax.random.uniform(row_key, shape[:-1] + (1,), jnp.float32, -1.15, 1.15))
    base = jax.random.normal(base_key, shape, jnp.float32)
    return jnp.clip(base * row_scale * column_scale / 1.5, -12.0, 12.0)


def draw_waiting(key, part):
    return spread_rows(jax.random.fold_in(key, 101), (N_SECTION, TOKP, D)).astype(jnp.bfloat16)


def draw_entering(key, part):
    return spread_rows(jax.random.fold_in(key, 202), (TICKS - 1, TOKP, D)).astype(jnp.bfloat16)


def level_of(rng, extent, cuts, least, top_value):
    level, own = 1.0, jax.random.fold_in(rng, 6)
    for axis_at, parts in cuts:
        steps = jnp.exp(jax.random.uniform(jax.random.fold_in(own, axis_at), (parts,), jnp.float32, least / len(cuts), top_value / len(cuts)))
        level = level * jnp.repeat(steps, extent[axis_at] // parts).reshape([-1 if axis == axis_at else 1 for axis in range(len(extent))])
    return level


def centred(own_key, extent, width, most, shards=(), kind=jnp.bfloat16):
    drawn = width * jax.random.normal(own_key, extent, jnp.float32)
    if shards:
        drawn = drawn * level_of(own_key, extent, shards, -0.22, 0.18)
    return jnp.clip(drawn, -most, most).astype(kind)


def setup_inputs(seed: int = 0) -> dict:
    streams_of = jax.random.split(jax.random.key(seed), 11)
    return {
        "waiting": draw_waiting(jax.random.fold_in(streams_of[10], 71), 0),
        "entering": draw_entering(jax.random.fold_in(streams_of[10], 71), 0),
        "patch_order": jax.random.permutation(streams_of[2], PATCHES).astype(jnp.int32),
        "step_index": jax.random.randint(streams_of[3], (1,), 0, STEPS).astype(jnp.int32),
        "modulation": centred(streams_of[4], (N_SECTION, STEPS, 3, D), 0.7, 4.0, ((0, 16),), jnp.float32),
        "projection": centred(streams_of[5], (N_SECTION, D, 3, HEADS * HD), D ** -0.5, 0.109375, ((0, 16), (3, 16))),
        "key_gain": jnp.clip(jnp.exp(math.log(3.0) - 0.4054651 * jax.random.uniform(streams_of[6], (N_SECTION, HEADS * HD), jnp.float32) ** level_of(streams_of[6], (N_SECTION, HEADS * HD), ((0, 16), (1, 16)), -0.2, 0.2)), 2.0, 3.0),
        "output_weight": centred(streams_of[7], (N_SECTION, HEADS * HD, D), (HEADS * HD) ** -0.5, 0.125, ((0, 16), (1, 16))),
        "stale_keys": jnp.clip(jax.random.uniform(streams_of[8], (N_SECTION, PATCHES, TOKP, HEADS * HD), jnp.float32, -4.0, 4.0) * level_of(streams_of[8], (N_SECTION, PATCHES, TOKP, HEADS * HD), ((0, 16), (3, 16)), -0.4, 0.0), -4.0, 4.0).astype(jnp.bfloat16),
        "stale_values": centred(streams_of[9], (N_SECTION, PATCHES, TOKP, HEADS * HD), 1.0, 4.0, ((0, 16), (3, 16))),
    }


epsilon = 1e-06

def root_norm(tensor):
    return tensor / jnp.sqrt(lax.optimization_barrier(jnp.mean(tensor * tensor, axis=-1, keepdims=True)) + epsilon)

def one_head(operands):
    head_q, head_k, head_v = operands
    logits = jnp.dot(head_q, head_k.T, preferred_element_type=jnp.float32) * HD ** (-0.5)
    exponent = jnp.exp(logits)
    weights = (exponent / lax.optimization_barrier(jnp.sum(exponent, axis=-1, keepdims=True))).astype(jnp.bfloat16)
    return jnp.dot(weights, head_v, preferred_element_type=jnp.float32).astype(jnp.bfloat16)

def run_layer(inflow, modulate, flat_weight, key_scale, cache_k, cache_v, patch_slot, out_matrix):
    tokens = inflow.shape[0]
    inflow_wide = inflow.astype(jnp.float32)
    normed = (root_norm(inflow_wide) * (1.0 + modulate[1]) + modulate[0]).astype(jnp.bfloat16)
    projected = jnp.dot(normed, flat_weight, preferred_element_type=jnp.float32).reshape(tokens, 3, HEADS, HD)
    queries = root_norm(projected[:, 0]).astype(jnp.bfloat16)
    keys_new = (root_norm(projected[:, 1]) * key_scale).astype(jnp.bfloat16)
    values_new = projected[:, 2].astype(jnp.bfloat16)
    anchor = jnp.zeros((), jnp.int32)
    corner = (patch_slot.astype(jnp.int32), anchor, anchor)
    cache_k = lax.dynamic_update_slice(cache_k, keys_new.reshape(1, tokens, HEADS * HD), corner)
    cache_v = lax.dynamic_update_slice(cache_v, values_new.reshape(1, tokens, HEADS * HD), corner)
    keys_heads = cache_k.reshape(PATCHES * tokens, HEADS, HD).transpose(1, 0, 2)
    values_heads = cache_v.reshape(PATCHES * tokens, HEADS, HD).transpose(1, 0, 2)
    attended = lax.map(one_head, (queries.transpose(1, 0, 2), keys_heads, values_heads))
    attended = attended.transpose(1, 0, 2).reshape(tokens, HEADS * HD)
    groups = N_BLK
    group_width = HEADS * HD // N_BLK
    partials = jnp.einsum('ngc,gcd->gnd', attended.reshape(tokens, groups, group_width).astype(jnp.float32), out_matrix.reshape(groups, group_width, D).astype(jnp.float32))
    rounded = lax.optimization_barrier(partials.astype(jnp.bfloat16)).astype(jnp.float32)
    attention = lax.optimization_barrier(jnp.sum(rounded, axis=0))
    produced = (inflow_wide + modulate[2] * attention).astype(jnp.bfloat16)
    fresh_pair = jnp.stack([keys_new.reshape(tokens, HEADS * HD), values_new.reshape(tokens, HEADS * HD)], axis=1)
    return (produced, fresh_pair, cache_k, cache_v)

def reference(waiting, entering, patch_order, step_index, modulation, projection, key_gain, output_weight, stale_keys, stale_values):
    tokens = waiting.shape[1]
    queued = jnp.concatenate([entering, jnp.zeros((1, tokens, D), entering.dtype)], axis=0)
    sections = jnp.arange(N_SECTION, dtype=jnp.int32)

    def section_pass(previous, operands):
        start_rows, mod_table, layer_weight, gain_row, out_matrix, cache_k, cache_v, section_index = operands
        modulate = lax.dynamic_index_in_dim(mod_table, step_index[0], 0, keepdims=False)
        flat_weight = layer_weight.reshape(D, 3 * HEADS * HD)
        key_scale = gain_row.reshape(HEADS, HD)
        produced_rows = []
        fresh_rows = []
        for tick_index in range(TICKS):
            inflow = start_rows if tick_index == 0 else previous[tick_index - 1]
            position = jnp.mod(tick_index - section_index, PATCHES).astype(jnp.int32)
            patch_slot = lax.dynamic_index_in_dim(patch_order, position, 0, keepdims=False)
            produced, fresh_pair, cache_k, cache_v = run_layer(inflow, modulate, flat_weight, key_scale, cache_k, cache_v, patch_slot, out_matrix)
            produced_rows.append(produced)
            fresh_rows.append(fresh_pair)
        stacked = jnp.stack(produced_rows)
        return (stacked, (stacked, jnp.stack(fresh_rows)))
    _, (layer_out, fresh_kv) = lax.scan(section_pass, queued, (waiting, modulation, projection, key_gain, output_weight, stale_keys, stale_values, sections))
    return (layer_out, fresh_kv)
```

```python
import functools
import math

import jax
import jax.numpy as jnp
from jax import lax
from jax.experimental import pallas as pl
from jax.experimental.pallas import tpu as pltpu
from jax.sharding import PartitionSpec as P

D = 3072
HD = 128
PATCHES = 12
TICKS = 4
TOKP = 512
ROWS = 32
BLOCKS = 8
HALF = BLOCKS * ROWS

epsilon = 1e-06
EXP2_SCALE = HD ** (-0.5) * math.log2(math.e)

VMEM = pl.BlockSpec(memory_space=pltpu.VMEM)
SMEM = pl.BlockSpec(memory_space=pltpu.SMEM)


def params(mib):
    return pltpu.CompilerParams(vmem_limit_bytes=mib * 1024 * 1024)


def shift(x, dy, dx, dc):
    pairs = []
    for y in range(2):
        for a in range(4):
            for c in range(2):
                target = (((y + dy) % 2) * 4 + (a + dx) % 4) * 2 + (c + dc) % 2
                pairs.append(((y * 4 + a) * 2 + c, target))
    return lax.ppermute(x, "blk", pairs)


def passed_along(x, axis, by):
    size = lax.axis_size(axis)
    pairs = [(i, i + by) for i in range(size) if 0 <= i + by < size]
    return lax.ppermute(x, axis, pairs)


def normalized(t):
    return t / jnp.sqrt(jnp.mean(t * t, axis=-1, keepdims=True) + epsilon)


def norm_kernel(first_ref, entering_ref, passed_ref, modulate_ref, inflow_ref, normed_ref):
    first = jnp.full((ROWS, D), first_ref[0], jnp.int32) == 1
    inflow = jnp.where(first, entering_ref[...].astype(jnp.float32), passed_ref[...].astype(jnp.float32))
    inflow_ref[...] = inflow.astype(jnp.bfloat16)
    normed = normalized(inflow) * (1.0 + modulate_ref[1:2, :]) + modulate_ref[0:1, :]
    normed_ref[...] = normed.astype(jnp.bfloat16)


def norm_call(first, entering, passed, modulate):
    shape = jax.ShapeDtypeStruct((ROWS, D), jnp.bfloat16)
    return pl.pallas_call(
        norm_kernel,
        out_shape=(shape, shape),
        in_specs=[SMEM, VMEM, VMEM, VMEM],
        out_specs=(VMEM, VMEM),
        compiler_params=params(8),
        cost_estimate=pl.CostEstimate(flops=10 * ROWS * D, bytes_accessed=10 * ROWS * D, transcendentals=0),
        name="norm",
    )(first, entering, passed, modulate)


def project_kernel(*refs):
    blocks, (weight_ref, gain_ref, q_ref, kv_ref) = refs[:BLOCKS], refs[BLOCKS:]
    x = jnp.concatenate([b[...] for b in blocks], axis=0)
    for head in range(2):
        out = jnp.dot(x, weight_ref[:, head * 384:(head + 1) * 384], preferred_element_type=jnp.float32)
        q_ref[head] = normalized(out[:, :128]).astype(jnp.bfloat16)
        kv_ref[head, 0] = (normalized(out[:, 128:256]) * gain_ref[head:head + 1, :]).astype(jnp.bfloat16)
        kv_ref[head, 1] = out[:, 256:].astype(jnp.bfloat16)


def project_call(blocks, weight, gain):
    return pl.pallas_call(
        project_kernel,
        out_shape=(
            jax.ShapeDtypeStruct((2, HALF, HD), jnp.bfloat16),
            jax.ShapeDtypeStruct((2, 2, HALF, HD), jnp.bfloat16),
        ),
        in_specs=[VMEM] * (BLOCKS + 2),
        out_specs=(VMEM, VMEM),
        compiler_params=params(24),
        cost_estimate=pl.CostEstimate(flops=2 * HALF * D * 768, bytes_accessed=2 * (D * 768 + HALF * D), transcendentals=0),
        name="project",
    )(*blocks, weight, gain)


def attend(q, k, v):
    logits = lax.dot_general(q, k, (((1,), (1,)), ((), ())), preferred_element_type=jnp.float32)
    exponent = jnp.exp2(logits * EXP2_SCALE).astype(jnp.bfloat16)
    wide = jnp.concatenate([v, jnp.ones_like(v)], axis=1)
    return jnp.dot(exponent, wide, preferred_element_type=jnp.float32)


def stale_kernel(tick, slots_ref, q_ref, own_k, own_v, other_k, other_v, *refs):
    fresh, total_ref = refs[:-1], refs[-1]
    for head, (k_ref, v_ref) in enumerate(((own_k, own_v), (other_k, other_v))):
        q = q_ref[head]
        total = jnp.zeros((HALF, 2 * HD), jnp.float32)
        for j in range(tick + 1, PATCHES):
            slot = slots_ref[j]
            total += attend(q, k_ref[slot], v_ref[slot])
        for index, ref in enumerate(fresh):
            at = head if index % 2 == 0 else 1 - head
            total += attend(q, ref[at, 0], ref[at, 1])
        total_ref[head] = total


def stale_call(tick, slots, q, caches, fresh):
    keys = TOKP * (PATCHES - 1 - tick) + HALF * len(fresh)
    return pl.pallas_call(
        functools.partial(stale_kernel, tick),
        out_shape=jax.ShapeDtypeStruct((2, HALF, 2 * HD), jnp.float32),
        in_specs=[SMEM] + [VMEM] * (5 + len(fresh)),
        out_specs=VMEM,
        compiler_params=params(24),
        cost_estimate=pl.CostEstimate(flops=16 * HALF * keys * HD, bytes_accessed=8 * keys * HD, transcendentals=2 * HALF * keys),
        name="stale",
    )(slots, q, *caches, *fresh)


def fresh_kernel(q_ref, kv_ref, total_ref, attended_ref):
    for head in range(2):
        total = total_ref[head] + attend(q_ref[head], kv_ref[1 - head, 0], kv_ref[1 - head, 1])
        attended = (total[:, :HD] / total[:, HD:]).astype(jnp.bfloat16)
        attended_ref[:, :, head * HD:(head + 1) * HD] = attended.reshape(4, 2 * ROWS, HD)


def fresh_call(q, kv, total):
    return pl.pallas_call(
        fresh_kernel,
        out_shape=jax.ShapeDtypeStruct((4, 2 * ROWS, 2 * HD), jnp.bfloat16),
        in_specs=[VMEM] * 3,
        out_specs=VMEM,
        compiler_params=params(16),
        cost_estimate=pl.CostEstimate(flops=16 * HALF * HALF * HD, bytes_accessed=8 * HALF * HALF, transcendentals=2 * HALF * HALF),
        name="fresh",
    )(q, kv, total)


def output_kernel(a0, a1, a2, a3, w0, w1, w2, w3, u0, u1, u2, u3, own_ref, other_ref):
    total = None
    for a, w, u in ((a0, w0, u0), (a1, w1, u1), (a2, w2, u2), (a3, w3, u3)):
        weight = jnp.concatenate([w[...], u[...]], axis=0)
        part = jnp.dot(a[...], weight, preferred_element_type=jnp.float32)
        total = part if total is None else total + part
    own_ref[...] = total[:ROWS]
    other_ref[...] = total[ROWS:].astype(jnp.bfloat16)


def output_call(parts, own_weights, other_weights):
    return pl.pallas_call(
        output_kernel,
        out_shape=(jax.ShapeDtypeStruct((ROWS, D), jnp.float32), jax.ShapeDtypeStruct((ROWS, D), jnp.bfloat16)),
        in_specs=[VMEM] * 12,
        out_specs=(VMEM, VMEM),
        compiler_params=params(24),
        cost_estimate=pl.CostEstimate(flops=2 * 2 * ROWS * 8 * HD * D, bytes_accessed=2 * 8 * HD * D, transcendentals=0),
        name="output",
    )(*parts, *own_weights, *other_weights)


def finish_kernel(inflow_ref, own_ref, other_ref, modulate_ref, out_ref):
    attention = own_ref[...] + other_ref[...].astype(jnp.float32)
    out_ref[...] = (inflow_ref[...].astype(jnp.float32) + modulate_ref[2:3, :] * attention).astype(jnp.bfloat16)


def finish_call(inflow, own, other, modulate):
    return pl.pallas_call(
        finish_kernel,
        out_shape=jax.ShapeDtypeStruct((ROWS, D), jnp.bfloat16),
        in_specs=[VMEM] * 4,
        out_specs=VMEM,
        compiler_params=params(8),
        cost_estimate=pl.CostEstimate(flops=4 * ROWS * D, bytes_accessed=10 * ROWS * D, transcendentals=0),
        name="finish",
    )(inflow, own, other, modulate)


def body(
    waiting,
    entering,
    patch_order,
    step_index,
    modulation,
    projection,
    key_gain,
    output_weight,
    stale_keys,
    stale_values,
):
    section = lax.axis_index("section")
    blk = lax.axis_index("blk")
    core, x_at, y_at = blk % 2, (blk // 2) % 4, blk // 8
    modulate = lax.dynamic_index_in_dim(modulation[0], step_index[0], 0, keepdims=False)
    slots = patch_order[jnp.mod(jnp.arange(PATCHES, dtype=jnp.int32) - section, PATCHES)]
    first = (section == 0).astype(jnp.int32).reshape(1)

    def gathered(normed):
        xm = shift(normed, 0, 1, 0)
        xp = shift(normed, 0, -1, 0)
        y0 = shift(normed, 1, 0, 0)
        x2 = shift(normed, 0, 2, 0)
        ym = shift(y0, 0, 1, 0)
        yp = shift(y0, 0, -1, 0)
        y2 = shift(x2, 1, 0, 0)
        return [normed, y0, xp, yp, x2, y2, xm, ym]

    inflow, normed = norm_call(jnp.zeros((1,), jnp.int32), waiting[0], waiting[0], modulate)
    blocks = gathered(normed)
    flat = projection[0].transpose(1, 0, 2)
    flat_other = shift(flat, 0, 0, 1)
    weight = jnp.concatenate([flat, flat_other], axis=0).transpose(1, 0, 2).reshape(D, 6 * HD)
    gain = jnp.concatenate([key_gain, shift(key_gain, 0, 0, 1)], axis=0)
    caches = (stale_keys[0], stale_values[0])
    caches = caches + tuple(shift(c, 0, 0, 1) for c in caches)
    out_own = output_weight[0]
    own_weights = [out_own] + [shift(out_own, 0, -dx, 0) for dx in (1, 2, 3)]
    other_weights = [shift(w, 0, 0, 1) for w in own_weights]

    fresh = []
    produced_rows = []
    fresh_rows = []
    for tick in range(TICKS):
        if tick > 0:
            passed = passed_along(produced_rows[-1], "section", 1)
            inflow, normed = norm_call(first, entering[tick - 1], passed, modulate)
            blocks = gathered(normed)
        q, kv = project_call(blocks, weight, gain)
        received = shift(kv, 0, 0, 1)
        total = stale_call(tick, slots, q, caches, fresh + [kv])
        attended = fresh_call(q, received, total)
        fresh = fresh + [kv, received]
        parts = [attended[0]] + [shift(attended[4 - dx], 0, -dx, 0) for dx in (1, 2, 3)]
        own, other = output_call(parts, own_weights, other_weights)
        current = finish_call(inflow, own, shift(other, 1, 0, 0), modulate)
        produced_rows.append(current)
        mine, theirs = kv[0], received[1]
        pair = jnp.stack([jnp.where(core == 0, mine, theirs), jnp.where(core == 0, theirs, mine)])
        pair = pair.reshape(2, 2, 4, 2, ROWS, HD)
        pair = jnp.where(y_at == 0, pair, pair[:, :, :, ::-1])
        double = jnp.concatenate([pair, pair[:, :, :3]], axis=2)
        pair = lax.dynamic_slice_in_dim(double, jnp.mod(4 - x_at, 4), 4, axis=2)
        fresh_rows.append(pair.transpose(3, 2, 0, 4, 1, 5).reshape(TOKP, 2, HD))
    layer_out = jnp.stack(produced_rows)[None]
    fresh_kv = jnp.stack(fresh_rows)[None]
    return (layer_out, fresh_kv)


def solution(mesh):
    placed = (
        P("section", "blk", None),
        P(None, "blk", None),
        P(),
        P(),
        P("section", None, None, None),
        P("section", None, None, "blk"),
        P("section", "blk"),
        P("section", "blk", None),
        P("section", None, None, "blk"),
        P("section", None, None, "blk"),
    )
    return jax.shard_map(
        body,
        mesh=mesh,
        in_specs=placed,
        out_specs=(P("section", None, "blk", None), P("section", None, None, None, "blk")),
        check_vma=False,
    )
```

```python
import functools
import math

import jax
import jax.numpy as jnp
from jax import lax
from jax.experimental import pallas as pl
from jax.experimental.pallas import tpu as pltpu
from jax.sharding import PartitionSpec as P

D = 3072
HD = 128
PATCHES = 12
TICKS = 4
TOKP = 512
ROWS = 32
BLOCKS = 8
HALF = BLOCKS * ROWS
CHUNK = HALF // 2

epsilon = 1e-06
EXP2_SCALE = HD ** (-0.5) * math.log2(math.e)

VMEM = pl.BlockSpec(memory_space=pltpu.VMEM)
SMEM = pl.BlockSpec(memory_space=pltpu.SMEM)


def params(mib):
    return pltpu.CompilerParams(vmem_limit_bytes=mib * 1024 * 1024)


def shift(x, dy, dx, dc):
    pairs = []
    for y in range(2):
        for a in range(4):
            for c in range(2):
                target = (((y + dy) % 2) * 4 + (a + dx) % 4) * 2 + (c + dc) % 2
                pairs.append(((y * 4 + a) * 2 + c, target))
    return lax.ppermute(x, "blk", pairs)


def passed_along(x, axis, by):
    size = lax.axis_size(axis)
    pairs = [(i, i + by) for i in range(size) if 0 <= i + by < size]
    return lax.ppermute(x, axis, pairs)


def normalized(t):
    return t / jnp.sqrt(jnp.mean(t * t, axis=-1, keepdims=True) + epsilon)


def norm_kernel(first_ref, entering_ref, passed_ref, modulate_ref, inflow_ref, normed_ref):
    first = jnp.full((ROWS, D), first_ref[0], jnp.int32) == 1
    inflow = jnp.where(first, entering_ref[...].astype(jnp.float32), passed_ref[...].astype(jnp.float32))
    inflow_ref[...] = inflow.astype(jnp.bfloat16)
    normed = normalized(inflow) * (1.0 + modulate_ref[1:2, :]) + modulate_ref[0:1, :]
    normed_ref[...] = normed.astype(jnp.bfloat16)


def norm_call(first, entering, passed, modulate):
    shape = jax.ShapeDtypeStruct((ROWS, D), jnp.bfloat16)
    return pl.pallas_call(
        norm_kernel,
        out_shape=(shape, shape),
        in_specs=[SMEM, VMEM, VMEM, VMEM],
        out_specs=(VMEM, VMEM),
        compiler_params=params(8),
        cost_estimate=pl.CostEstimate(flops=10 * ROWS * D, bytes_accessed=10 * ROWS * D, transcendentals=0),
        name="norm",
    )(first, entering, passed, modulate)


def pack_kernel(own_ref, other_ref, out_ref):
    for part in range(3):
        out_ref[:, part * HD:(part + 1) * HD] = own_ref[part]
        out_ref[:, (3 + part) * HD:(4 + part) * HD] = other_ref[part]


def pack_call(own, other):
    return pl.pallas_call(
        pack_kernel,
        out_shape=jax.ShapeDtypeStruct((D, 6 * HD), jnp.bfloat16),
        grid=(4,),
        in_specs=[pl.BlockSpec((3, D // 4, HD), lambda i: (0, i, 0))] * 2,
        out_specs=pl.BlockSpec((D // 4, 6 * HD), lambda i: (i, 0)),
        compiler_params=params(12),
        cost_estimate=pl.CostEstimate(flops=0, bytes_accessed=4 * D * 6 * HD, transcendentals=0),
        name="pack",
    )(own, other)


def project_kernel(*refs):
    blocks, (weight_ref, gain_ref, q_ref, kv_ref) = refs[:4], refs[4:]
    x = jnp.concatenate([b[...] for b in blocks], axis=0)
    out = jnp.dot(x, weight_ref[...], preferred_element_type=jnp.float32)
    for head in range(2):
        at = head * 3 * HD
        q_ref[head] = normalized(out[:, at:at + HD]).astype(jnp.bfloat16)
        k = normalized(out[:, at + HD:at + 2 * HD]) * gain_ref[head:head + 1, :]
        kv_ref[head, 0] = k.astype(jnp.bfloat16)
        kv_ref[head, 1] = out[:, at + 2 * HD:at + 3 * HD].astype(jnp.bfloat16)


def project_call(blocks, weight, gain):
    return pl.pallas_call(
        project_kernel,
        out_shape=(
            jax.ShapeDtypeStruct((2, CHUNK, HD), jnp.bfloat16),
            jax.ShapeDtypeStruct((2, 2, CHUNK, HD), jnp.bfloat16),
        ),
        in_specs=[VMEM] * 6,
        out_specs=(VMEM, VMEM),
        compiler_params=params(12),
        cost_estimate=pl.CostEstimate(flops=2 * CHUNK * D * 768, bytes_accessed=2 * (D * 768 + CHUNK * D), transcendentals=0),
        name="project",
    )(*blocks, weight, gain)


def attend(q, k, v):
    logits = lax.dot_general(q, k, (((1,), (1,)), ((), ())), preferred_element_type=jnp.float32)
    exponent = jnp.exp2(logits * EXP2_SCALE).astype(jnp.bfloat16)
    wide = jnp.concatenate([v, jnp.ones_like(v)], axis=1)
    return jnp.dot(exponent, wide, preferred_element_type=jnp.float32)


def stale_kernel(tick, slots_ref, q_ref, own_k, own_v, other_k, other_v, *refs):
    fresh, total_ref = refs[:-1], refs[-1]
    for head, (k_ref, v_ref) in enumerate(((own_k, own_v), (other_k, other_v))):
        q = q_ref[head]
        total = jnp.zeros((CHUNK, 2 * HD), jnp.float32)
        for j in range(tick + 1, PATCHES):
            slot = slots_ref[j]
            total += attend(q, k_ref[slot], v_ref[slot])
        for ref in fresh:
            total += attend(q, ref[head, 0], ref[head, 1])
        total_ref[head] = total


def stale_call(tick, slots, q, caches, fresh):
    keys = TOKP * (PATCHES - 1)
    return pl.pallas_call(
        functools.partial(stale_kernel, tick),
        out_shape=jax.ShapeDtypeStruct((2, CHUNK, 2 * HD), jnp.float32),
        in_specs=[SMEM] + [VMEM] * (5 + len(fresh)),
        out_specs=VMEM,
        compiler_params=params(20),
        cost_estimate=pl.CostEstimate(flops=16 * CHUNK * keys * HD, bytes_accessed=8 * keys * HD, transcendentals=2 * CHUNK * keys),
        name="stale",
    )(slots, q, *caches, *fresh)


CHUNKS = (((0, 0), (0, 1), (1, 0), (3, 0)), ((2, 0), (1, 1), (3, 1), (2, 1)))


def fresh_kernel(place_ref, qa, qb, ta, tb, kva, rxa, kvb, rxb, kept_ref, sent_ref, kv_ref):
    y_at, x_at, core = place_ref[0], place_ref[1], place_ref[2]
    for index, (mine, theirs) in enumerate(((kva, rxa), (kvb, rxb))):
        for n, (dx, dy) in enumerate(CHUNKS[index]):
            chip = lax.rem(y_at + dy, 2) * 4 + lax.rem(x_at + dx, 4)
            rows = pl.ds(n * ROWS, ROWS)
            here = pl.ds(pl.multiple_of((chip * 2 + core) * ROWS, ROWS), ROWS)
            there = pl.ds(pl.multiple_of((chip * 2 + 1 - core) * ROWS, ROWS), ROWS)
            for head in range(2):
                for part in range(2):
                    kv_ref[head, part, here, :] = mine[head, part, rows, :]
                    kv_ref[head, part, there, :] = theirs[1 - head, part, rows, :]
    for head in range(2):
        q = jnp.concatenate([qa[head], qb[head]], axis=0)
        total = jnp.concatenate([ta[head], tb[head]], axis=0)
        for mine, theirs in ((kva, rxa), (kvb, rxb)):
            k = jnp.concatenate([mine[head, 0], theirs[1 - head, 0]], axis=0)
            v = jnp.concatenate([mine[head, 1], theirs[1 - head, 1]], axis=0)
            total += attend(q, k, v)
        attended = (total[:, :HD] / total[:, HD:]).astype(jnp.bfloat16)
        for n, (dx, dy) in enumerate(CHUNKS[0] + CHUNKS[1]):
            target = sent_ref if dy else kept_ref
            target[dx, :, head * HD:(head + 1) * HD] = attended[n * ROWS:(n + 1) * ROWS]


def fresh_call(place, queries, totals, kvs, received):
    rows = jax.ShapeDtypeStruct((4, ROWS, 2 * HD), jnp.bfloat16)
    return pl.pallas_call(
        fresh_kernel,
        out_shape=(rows, rows, jax.ShapeDtypeStruct((2, 2, TOKP, HD), jnp.bfloat16)),
        in_specs=[SMEM] + [VMEM] * 8,
        out_specs=(VMEM, VMEM, VMEM),
        compiler_params=params(12),
        cost_estimate=pl.CostEstimate(flops=16 * HALF * TOKP * HD, bytes_accessed=8 * TOKP * HD, transcendentals=2 * HALF * TOKP),
        name="fresh",
    )(place, *queries, *totals, kvs[0], received[0], kvs[1], received[1])


def output_kernel(kept_ref, got_ref, w0, w1, w2, w3, own_ref, p1_ref, p2_ref, p3_ref):
    total = None
    for a_ref, w, u in ((kept_ref, w0, w1), (got_ref, w2, w3)):
        a = jnp.concatenate([a_ref[dx] for dx in range(4)], axis=0)
        weight = jnp.concatenate([w[...], u[...]], axis=0)
        part = jnp.dot(a, weight, preferred_element_type=jnp.float32)
        total = part if total is None else total + part
    own_ref[...] = total[:ROWS]
    for dx, ref in ((1, p1_ref), (2, p2_ref), (3, p3_ref)):
        ref[...] = total[dx * ROWS:(dx + 1) * ROWS].astype(jnp.bfloat16)


def output_call(kept, got, weights):
    part = jax.ShapeDtypeStruct((ROWS, D), jnp.bfloat16)
    return pl.pallas_call(
        output_kernel,
        out_shape=(jax.ShapeDtypeStruct((ROWS, D), jnp.float32), part, part, part),
        in_specs=[VMEM] * 6,
        out_specs=(VMEM,) * 4,
        compiler_params=params(12),
        cost_estimate=pl.CostEstimate(flops=2 * 4 * ROWS * 4 * HD * D, bytes_accessed=2 * 4 * HD * D, transcendentals=0),
        name="output",
    )(kept, got, *weights)


def finished(inflow_ref, own_ref, p1_ref, p2_ref, p3_ref, modulate_ref):
    attention = own_ref[...]
    for ref in (p1_ref, p2_ref, p3_ref):
        attention += ref[...].astype(jnp.float32)
    return (inflow_ref[...].astype(jnp.float32) + modulate_ref[2:3, :] * attention).astype(jnp.bfloat16)


def finish_kernel(*refs):
    refs[-1][...] = finished(*refs[:-1])


def finish_call(inflow, own, parts, modulate):
    return pl.pallas_call(
        finish_kernel,
        out_shape=jax.ShapeDtypeStruct((ROWS, D), jnp.bfloat16),
        in_specs=[VMEM] * 6,
        out_specs=VMEM,
        compiler_params=params(8),
        cost_estimate=pl.CostEstimate(flops=6 * ROWS * D, bytes_accessed=14 * ROWS * D, transcendentals=0),
        name="finish",
    )(inflow, own, *parts, modulate)


def last_kernel(*refs):
    out_ref, rows, stored = refs[-3:]
    rows[...] = finished(*refs[:6])
    copy = pltpu.make_async_copy(rows, out_ref.at[TICKS - 1], stored)
    copy.start()
    copy.wait()


def last_call(inflow, own, parts, modulate, whole):
    anywhere = pl.BlockSpec(memory_space=pl.ANY)
    return pl.pallas_call(
        last_kernel,
        out_shape=jax.ShapeDtypeStruct((TICKS, ROWS, D), jnp.bfloat16),
        in_specs=[VMEM] * 6 + [anywhere],
        out_specs=anywhere,
        scratch_shapes=[pltpu.VMEM((ROWS, D), jnp.bfloat16), pltpu.SemaphoreType.DMA],
        input_output_aliases={6: 0},
        compiler_params=params(8),
        cost_estimate=pl.CostEstimate(flops=6 * ROWS * D, bytes_accessed=14 * ROWS * D, transcendentals=0),
        name="last",
    )(inflow, own, *parts, modulate, whole)


def body(
    waiting,
    entering,
    patch_order,
    step_index,
    modulation,
    projection,
    key_gain,
    output_weight,
    stale_keys,
    stale_values,
):
    section = lax.axis_index("section")
    blk = lax.axis_index("blk")
    place = jnp.stack([blk // 8, (blk // 2) % 4, blk % 2]).astype(jnp.int32)
    modulate = lax.dynamic_index_in_dim(modulation[0], step_index[0], 0, keepdims=False)
    positions = jnp.mod(jnp.arange(PATCHES, dtype=jnp.int32) - section, PATCHES)
    slots = jnp.sum(jnp.where(positions[:, None] == jnp.arange(PATCHES)[None, :], patch_order[None, :], 0), axis=1)
    first = (section == 0).astype(jnp.int32).reshape(1)

    flat = projection[0].transpose(1, 0, 2)
    flat_other = shift(flat, 0, 0, 1)
    gain = jnp.concatenate([key_gain, shift(key_gain, 0, 0, 1)], axis=0)

    fresh = []
    produced_rows = []
    fresh_rows = []
    for tick in range(TICKS):
        if tick == 0:
            inflow, normed = norm_call(jnp.zeros((1,), jnp.int32), waiting[0], waiting[0], modulate)
        else:
            passed = passed_along(produced_rows[-1], "section", 1)
            inflow, normed = norm_call(first, entering[tick - 1], passed, modulate)
        xm = shift(normed, 0, 1, 0)
        xp = shift(normed, 0, -1, 0)
        y0 = shift(normed, 1, 0, 0)
        x2 = shift(normed, 0, 2, 0)
        ym = shift(y0, 0, 1, 0)
        yp = shift(y0, 0, -1, 0)
        if tick == 0:
            own_caches, _ = lax.optimization_barrier(((stale_keys[0], stale_values[0]), (xm, xp, y0)))
            caches = own_caches + tuple(shift(c, 0, 0, 1) for c in own_caches)
            weight = pack_call(flat, flat_other)
            y2 = shift(y0, 0, 2, 0)
            out_own, _ = lax.optimization_barrier((output_weight[0], (xm, xp, y0)))
            out_across = shift(out_own, 1, 0, 0)
            weights = (out_own, shift(out_own, 0, 0, 1), out_across)
        else:
            y2 = shift(x2, 1, 0, 0)
        queries, kvs, received, totals = [], [], [], []
        for blocks in ((normed, y0, xp, xm), (x2, yp, ym, y2)):
            q, kv = project_call(blocks, weight, gain)
            queries.append(q)
            kvs.append(kv)
            received.append(shift(kv, 0, 0, 1))
            totals.append(stale_call(tick, slots, q, caches, fresh))
        kept, sent, kv_all = fresh_call(place, queries, totals, kvs, received)
        if tick == 0:
            out_across, _ = lax.optimization_barrier((out_across, kept))
            weights = weights + (shift(out_across, 0, 0, 1),)
        fresh.append(kv_all)
        fresh_rows.append(kv_all[0].transpose(1, 0, 2))
        own, p1, p2, p3 = output_call(kept, shift(sent, 1, 0, 0), weights)
        parts = (shift(p2, 0, 2, 0), shift(p1, 0, 1, 0), shift(p3, 0, 3, 0))
        if tick < TICKS - 1:
            produced_rows.append(finish_call(inflow, own, parts, modulate))
        else:
            whole = jnp.stack(produced_rows + [jnp.zeros_like(inflow)])
            layer_out = last_call(inflow, own, parts, modulate, whole)
    return (layer_out[None], jnp.stack(fresh_rows)[None])


def solution(mesh):
    placed = (
        P("section", "blk", None),
        P(None, "blk", None),
        P(),
        P(),
        P("section", None, None, None),
        P("section", None, None, "blk"),
        P("section", "blk"),
        P("section", "blk", None),
        P("section", None, None, "blk"),
        P("section", None, None, "blk"),
    )
    return jax.shard_map(
        body,
        mesh=mesh,
        in_specs=placed,
        out_specs=(P("section", None, "blk", None), P("section", None, None, None, "blk")),
        check_vma=False,
    )
```

```python
import functools
import math

import jax
import jax.numpy as jnp
from jax import lax
from jax.experimental import pallas as pl
from jax.experimental.pallas import tpu as pltpu
from jax.sharding import PartitionSpec as P

D = 3072
HD = 128
PATCHES = 12
TICKS = 4
TOKP = 512
ROWS = 32
BLOCKS = 8
HALF = BLOCKS * ROWS
CHUNK = HALF // 2

epsilon = 1e-06
EXP2_SCALE = HD ** (-0.5) * math.log2(math.e)

VMEM = pl.BlockSpec(memory_space=pltpu.VMEM)
SMEM = pl.BlockSpec(memory_space=pltpu.SMEM)


def params(mib):
    return pltpu.CompilerParams(vmem_limit_bytes=mib * 1024 * 1024)


def shift(x, dy, dx, dc):
    pairs = []
    for y in range(2):
        for a in range(4):
            for c in range(2):
                target = (((y + dy) % 2) * 4 + (a + dx) % 4) * 2 + (c + dc) % 2
                pairs.append(((y * 4 + a) * 2 + c, target))
    return lax.ppermute(x, "blk", pairs)


def passed_along(x, axis, by):
    size = lax.axis_size(axis)
    pairs = [(i, i + by) for i in range(size) if 0 <= i + by < size]
    return lax.ppermute(x, axis, pairs)


def normalized(t):
    return t / jnp.sqrt(jnp.mean(t * t, axis=-1, keepdims=True) + epsilon)


def norm_kernel(first_ref, entering_ref, passed_ref, modulate_ref, inflow_ref, normed_ref):
    first = jnp.full((ROWS, D), first_ref[0], jnp.int32) == 1
    inflow = jnp.where(first, entering_ref[...].astype(jnp.float32), passed_ref[...].astype(jnp.float32))
    inflow_ref[...] = inflow.astype(jnp.bfloat16)
    normed = normalized(inflow) * (1.0 + modulate_ref[1:2, :]) + modulate_ref[0:1, :]
    normed_ref[...] = normed.astype(jnp.bfloat16)


def norm_call(first, entering, passed, modulate):
    shape = jax.ShapeDtypeStruct((ROWS, D), jnp.bfloat16)
    return pl.pallas_call(
        norm_kernel,
        out_shape=(shape, shape),
        in_specs=[SMEM, VMEM, VMEM, VMEM],
        out_specs=(VMEM, VMEM),
        compiler_params=params(8),
        cost_estimate=pl.CostEstimate(flops=10 * ROWS * D, bytes_accessed=10 * ROWS * D, transcendentals=0),
        name="norm",
    )(first, entering, passed, modulate)


def pack_kernel(own_ref, other_ref, out_ref):
    for part in range(3):
        out_ref[:, part * HD:(part + 1) * HD] = own_ref[part]
        out_ref[:, (3 + part) * HD:(4 + part) * HD] = other_ref[part]


def pack_call(own, other):
    return pl.pallas_call(
        pack_kernel,
        out_shape=jax.ShapeDtypeStruct((D, 6 * HD), jnp.bfloat16),
        grid=(4,),
        in_specs=[pl.BlockSpec((3, D // 4, HD), lambda i: (0, i, 0))] * 2,
        out_specs=pl.BlockSpec((D // 4, 6 * HD), lambda i: (i, 0)),
        compiler_params=params(12),
        cost_estimate=pl.CostEstimate(flops=0, bytes_accessed=4 * D * 6 * HD, transcendentals=0),
        name="pack",
    )(own, other)


def project_kernel(*refs):
    blocks, (weight_ref, gain_ref, q_ref, kv_ref) = refs[:4], refs[4:]
    x = jnp.concatenate([b[...] for b in blocks], axis=0)
    out = jnp.dot(x, weight_ref[...], preferred_element_type=jnp.float32)
    for head in range(2):
        at = head * 3 * HD
        q_ref[head] = normalized(out[:, at:at + HD]).astype(jnp.bfloat16)
        k = normalized(out[:, at + HD:at + 2 * HD]) * gain_ref[head:head + 1, :]
        kv_ref[head, 0] = k.astype(jnp.bfloat16)
        kv_ref[head, 1] = out[:, at + 2 * HD:at + 3 * HD].astype(jnp.bfloat16)


def project_call(blocks, weight, gain):
    return pl.pallas_call(
        project_kernel,
        out_shape=(
            jax.ShapeDtypeStruct((2, CHUNK, HD), jnp.bfloat16),
            jax.ShapeDtypeStruct((2, 2, CHUNK, HD), jnp.bfloat16),
        ),
        in_specs=[VMEM] * 6,
        out_specs=(VMEM, VMEM),
        compiler_params=params(12),
        cost_estimate=pl.CostEstimate(flops=2 * CHUNK * D * 768, bytes_accessed=2 * (D * 768 + CHUNK * D), transcendentals=0),
        name="project",
    )(*blocks, weight, gain)


def attend(q, k, v):
    logits = lax.dot_general(q, k, (((1,), (1,)), ((), ())), preferred_element_type=jnp.float32)
    exponent = jnp.exp2(logits * EXP2_SCALE).astype(jnp.bfloat16)
    wide = jnp.concatenate([v, jnp.ones_like(v)], axis=1)
    return jnp.dot(exponent, wide, preferred_element_type=jnp.float32)


def stale_kernel(tick, slots_ref, q_ref, own_k, own_v, other_k, other_v, *refs):
    fresh, total_ref = refs[:-1], refs[-1]
    for head, (k_ref, v_ref) in enumerate(((own_k, own_v), (other_k, other_v))):
        q = q_ref[head]
        total = jnp.zeros((CHUNK, 2 * HD), jnp.float32)
        for j in range(tick + 1, PATCHES):
            slot = slots_ref[j]
            total += attend(q, k_ref[slot], v_ref[slot])
        for ref in fresh:
            total += attend(q, ref[head, 0], ref[head, 1])
        total_ref[head] = total


def stale_call(tick, slots, q, caches, fresh):
    keys = TOKP * (PATCHES - 1)
    return pl.pallas_call(
        functools.partial(stale_kernel, tick),
        out_shape=jax.ShapeDtypeStruct((2, CHUNK, 2 * HD), jnp.float32),
        in_specs=[SMEM] + [VMEM] * (5 + len(fresh)),
        out_specs=VMEM,
        compiler_params=params(20),
        cost_estimate=pl.CostEstimate(flops=16 * CHUNK * keys * HD, bytes_accessed=8 * keys * HD, transcendentals=2 * CHUNK * keys),
        name="stale",
    )(slots, q, *caches, *fresh)


def attended_rows(q_ref, t_ref, kvs, out_ref):
    for head in range(2):
        total = t_ref[head]
        for mine, theirs in kvs:
            k = jnp.concatenate([mine[head, 0], theirs[1 - head, 0]], axis=0)
            v = jnp.concatenate([mine[head, 1], theirs[1 - head, 1]], axis=0)
            total += attend(q_ref[head], k, v)
        attended = (total[:, :HD] / total[:, HD:]).astype(jnp.bfloat16)
        out_ref[:, :, head * HD:(head + 1) * HD] = attended.reshape(4, ROWS, HD)


def across_kernel(q_ref, t_ref, kva, rxa, kvb, rxb, out_ref):
    attended_rows(q_ref, t_ref, ((kva, rxa), (kvb, rxb)), out_ref)


def along_kernel(place_ref, q_ref, t_ref, kva, rxa, kvb, rxb, out_ref, kv_ref):
    attended_rows(q_ref, t_ref, ((kva, rxa), (kvb, rxb)), out_ref)
    y_at, x_at, core = place_ref[0], place_ref[1], place_ref[2]
    for dy, (mine, theirs) in enumerate(((kva, rxa), (kvb, rxb))):
        for dx in range(4):
            chip = lax.rem(y_at + dy, 2) * 4 + lax.rem(x_at + dx, 4)
            rows = pl.ds(dx * ROWS, ROWS)
            here = pl.ds(pl.multiple_of((chip * 2 + core) * ROWS, ROWS), ROWS)
            there = pl.ds(pl.multiple_of((chip * 2 + 1 - core) * ROWS, ROWS), ROWS)
            for head in range(2):
                for part in range(2):
                    kv_ref[head, part, here, :] = mine[head, part, rows, :]
                    kv_ref[head, part, there, :] = theirs[1 - head, part, rows, :]


FRESH_COST = pl.CostEstimate(
    flops=16 * CHUNK * TOKP * HD, bytes_accessed=8 * TOKP * HD, transcendentals=2 * CHUNK * TOKP
)


def across_call(q, total, kvs, received):
    return pl.pallas_call(
        across_kernel,
        out_shape=jax.ShapeDtypeStruct((4, ROWS, 2 * HD), jnp.bfloat16),
        in_specs=[VMEM] * 6,
        out_specs=VMEM,
        compiler_params=params(12),
        cost_estimate=FRESH_COST,
        name="across",
    )(q, total, kvs[0], received[0], kvs[1], received[1])


def along_call(place, q, total, kvs, received):
    return pl.pallas_call(
        along_kernel,
        out_shape=(
            jax.ShapeDtypeStruct((4, ROWS, 2 * HD), jnp.bfloat16),
            jax.ShapeDtypeStruct((2, 2, TOKP, HD), jnp.bfloat16),
        ),
        in_specs=[SMEM] + [VMEM] * 6,
        out_specs=(VMEM, VMEM),
        compiler_params=params(12),
        cost_estimate=FRESH_COST,
        name="along",
    )(place, q, total, kvs[0], received[0], kvs[1], received[1])


def output_kernel(kept_ref, got_ref, w0, w1, w2, w3, own_ref, p1_ref, p2_ref, p3_ref):
    total = None
    for a_ref, w, u in ((kept_ref, w0, w1), (got_ref, w2, w3)):
        a = jnp.concatenate([a_ref[dx] for dx in range(4)], axis=0)
        weight = jnp.concatenate([w[...], u[...]], axis=0)
        part = jnp.dot(a, weight, preferred_element_type=jnp.float32)
        total = part if total is None else total + part
    own_ref[...] = total[:ROWS]
    for dx, ref in ((1, p1_ref), (2, p2_ref), (3, p3_ref)):
        ref[...] = total[dx * ROWS:(dx + 1) * ROWS].astype(jnp.bfloat16)


def output_call(kept, got, weights):
    part = jax.ShapeDtypeStruct((ROWS, D), jnp.bfloat16)
    return pl.pallas_call(
        output_kernel,
        out_shape=(jax.ShapeDtypeStruct((ROWS, D), jnp.float32), part, part, part),
        in_specs=[VMEM] * 6,
        out_specs=(VMEM,) * 4,
        compiler_params=params(12),
        cost_estimate=pl.CostEstimate(flops=2 * 4 * ROWS * 4 * HD * D, bytes_accessed=2 * 4 * HD * D, transcendentals=0),
        name="output",
    )(kept, got, *weights)


def finished(inflow_ref, own_ref, p1_ref, p2_ref, p3_ref, modulate_ref):
    attention = own_ref[...]
    for ref in (p1_ref, p2_ref, p3_ref):
        attention += ref[...].astype(jnp.float32)
    return (inflow_ref[...].astype(jnp.float32) + modulate_ref[2:3, :] * attention).astype(jnp.bfloat16)


def finish_kernel(*refs):
    refs[-1][...] = finished(*refs[:-1])


def finish_call(inflow, own, parts, modulate):
    return pl.pallas_call(
        finish_kernel,
        out_shape=jax.ShapeDtypeStruct((ROWS, D), jnp.bfloat16),
        in_specs=[VMEM] * 6,
        out_specs=VMEM,
        compiler_params=params(8),
        cost_estimate=pl.CostEstimate(flops=6 * ROWS * D, bytes_accessed=14 * ROWS * D, transcendentals=0),
        name="finish",
    )(inflow, own, *parts, modulate)


def last_kernel(*refs):
    out_ref, rows, stored = refs[-3:]
    rows[...] = finished(*refs[:6])
    copy = pltpu.make_async_copy(rows, out_ref.at[TICKS - 1], stored)
    copy.start()
    copy.wait()


def last_call(inflow, own, parts, modulate, whole):
    anywhere = pl.BlockSpec(memory_space=pl.ANY)
    return pl.pallas_call(
        last_kernel,
        out_shape=jax.ShapeDtypeStruct((TICKS, ROWS, D), jnp.bfloat16),
        in_specs=[VMEM] * 6 + [anywhere],
        out_specs=anywhere,
        scratch_shapes=[pltpu.VMEM((ROWS, D), jnp.bfloat16), pltpu.SemaphoreType.DMA],
        input_output_aliases={6: 0},
        compiler_params=params(8),
        cost_estimate=pl.CostEstimate(flops=6 * ROWS * D, bytes_accessed=14 * ROWS * D, transcendentals=0),
        name="last",
    )(inflow, own, *parts, modulate, whole)


def body(
    waiting,
    entering,
    patch_order,
    step_index,
    modulation,
    projection,
    key_gain,
    output_weight,
    stale_keys,
    stale_values,
):
    section = lax.axis_index("section")
    blk = lax.axis_index("blk")
    place = jnp.stack([blk // 8, (blk // 2) % 4, blk % 2]).astype(jnp.int32)
    modulate = lax.dynamic_index_in_dim(modulation[0], step_index[0], 0, keepdims=False)
    positions = jnp.mod(jnp.arange(PATCHES, dtype=jnp.int32) - section, PATCHES)
    slots = jnp.sum(jnp.where(positions[:, None] == jnp.arange(PATCHES)[None, :], patch_order[None, :], 0), axis=1)
    first = (section == 0).astype(jnp.int32).reshape(1)

    gain = jnp.concatenate([key_gain, shift(key_gain, 0, 0, 1)], axis=0)
    flat = projection[0].transpose(1, 0, 2)
    flat_other = shift(flat, 0, 0, 1)

    fresh = []
    produced_rows = []
    fresh_rows = []
    for tick in range(TICKS):
        if tick == 0:
            inflow, normed = norm_call(jnp.zeros((1,), jnp.int32), waiting[0], waiting[0], modulate)
        else:
            passed = passed_along(produced_rows[-1], "section", 1)
            inflow, normed = norm_call(first, entering[tick - 1], passed, modulate)
        xm = shift(normed, 0, 1, 0)
        xp = shift(normed, 0, -1, 0)
        y0 = shift(normed, 1, 0, 0)
        x2 = shift(normed, 0, 2, 0)
        ym = shift(y0, 0, 1, 0)
        yp = shift(y0, 0, -1, 0)
        if tick == 0:
            y2 = shift(y0, 0, 2, 0)
            first_step = (xm, xp, y0, x2, flat_other)
            weight = pack_call(flat, flat_other)
            own_keys, _ = lax.optimization_barrier((stale_keys[0], first_step))
            other_keys = shift(own_keys, 0, 0, 1)
            own_values, _ = lax.optimization_barrier((stale_values[0], first_step))
            caches = (own_keys, own_values, other_keys, shift(own_values, 0, 0, 1))
            out_own, _ = lax.optimization_barrier((output_weight[0], (ym, yp)))
            out_across = shift(out_own, 1, 0, 0)
            weights = (out_own, shift(out_own, 0, 0, 1), out_across)
        else:
            y2 = shift(x2, 1, 0, 0)
        queries, kvs, received, totals = [], [], [], []
        for blocks in ((normed, xp, x2, xm), (y0, yp, y2, ym)):
            if totals:
                blocks, totals[0] = lax.optimization_barrier((blocks, totals[0]))
            q, kv = project_call(blocks, weight, gain)
            queries.append(q)
            kvs.append(kv)
            received.append(shift(kv, 0, 0, 1))
            totals.append(stale_call(tick, slots, q, caches, fresh))
        sent = across_call(queries[1], totals[1], kvs, received)
        kept, kv_all = along_call(place, queries[0], totals[0], kvs, received)
        if tick == 0:
            out_across, _ = lax.optimization_barrier((out_across, sent))
            weights = weights + (shift(out_across, 0, 0, 1),)
        fresh.append(kv_all)
        fresh_rows.append(kv_all[0].transpose(1, 0, 2))
        own, p1, p2, p3 = output_call(kept, shift(sent, 1, 0, 0), weights)
        parts = (shift(p2, 0, 2, 0), shift(p1, 0, 1, 0), shift(p3, 0, 3, 0))
        if tick < TICKS - 1:
            produced_rows.append(finish_call(inflow, own, parts, modulate))
        else:
            whole = jnp.stack(produced_rows + [jnp.zeros_like(inflow)])
            layer_out = last_call(inflow, own, parts, modulate, whole)
    return (layer_out[None], jnp.stack(fresh_rows)[None])


def solution(mesh):
    placed = (
        P("section", "blk", None),
        P(None, "blk", None),
        P(),
        P(),
        P("section", None, None, None),
        P("section", None, None, "blk"),
        P("section", "blk"),
        P("section", "blk", None),
        P("section", None, None, "blk"),
        P("section", None, None, "blk"),
    )
    return jax.shard_map(
        body,
        mesh=mesh,
        in_specs=placed,
        out_specs=(P("section", None, "blk", None), P("section", None, None, None, "blk")),
        check_vma=False,
    )
```

```python
import functools
import math

import jax
import jax.numpy as jnp
from jax import lax
from jax.experimental import pallas as pl
from jax.experimental.pallas import tpu as pltpu
from jax.sharding import PartitionSpec as P

D = 3072
HD = 128
PATCHES = 12
TICKS = 4
TOKP = 512
ROWS = 32
BLOCKS = 8
HALF = BLOCKS * ROWS
CHUNK = HALF // 2

epsilon = 1e-06
EXP2_SCALE = HD ** (-0.5) * math.log2(math.e)

VMEM = pl.BlockSpec(memory_space=pltpu.VMEM)
SMEM = pl.BlockSpec(memory_space=pltpu.SMEM)


def params(mib):
    return pltpu.CompilerParams(vmem_limit_bytes=mib * 1024 * 1024)


def shift(x, dy, dx, dc):
    pairs = []
    for y in range(2):
        for a in range(4):
            for c in range(2):
                target = (((y + dy) % 2) * 4 + (a + dx) % 4) * 2 + (c + dc) % 2
                pairs.append(((y * 4 + a) * 2 + c, target))
    return lax.ppermute(x, "blk", pairs)


def passed_along(x, axis, by):
    size = lax.axis_size(axis)
    pairs = [(i, i + by) for i in range(size) if 0 <= i + by < size]
    return lax.ppermute(x, axis, pairs)


def normalized(t):
    return t / jnp.sqrt(jnp.mean(t * t, axis=-1, keepdims=True) + epsilon)


def norm_kernel(first_ref, entering_ref, passed_ref, modulate_ref, inflow_ref, normed_ref):
    first = jnp.full((ROWS, D), first_ref[0], jnp.int32) == 1
    inflow = jnp.where(first, entering_ref[...].astype(jnp.float32), passed_ref[...].astype(jnp.float32))
    inflow_ref[...] = inflow.astype(jnp.bfloat16)
    normed = normalized(inflow) * (1.0 + modulate_ref[1:2, :]) + modulate_ref[0:1, :]
    normed_ref[...] = normed.astype(jnp.bfloat16)


def norm_call(first, entering, passed, modulate):
    shape = jax.ShapeDtypeStruct((ROWS, D), jnp.bfloat16)
    return pl.pallas_call(
        norm_kernel,
        out_shape=(shape, shape),
        in_specs=[SMEM, VMEM, VMEM, VMEM],
        out_specs=(VMEM, VMEM),
        compiler_params=params(8),
        cost_estimate=pl.CostEstimate(flops=10 * ROWS * D, bytes_accessed=10 * ROWS * D, transcendentals=0),
        name="norm",
    )(first, entering, passed, modulate)


def pack_kernel(own_ref, other_ref, out_ref):
    for part in range(3):
        out_ref[:, part * HD:(part + 1) * HD] = own_ref[part]
        out_ref[:, (3 + part) * HD:(4 + part) * HD] = other_ref[part]


def pack_call(own, other):
    return pl.pallas_call(
        pack_kernel,
        out_shape=jax.ShapeDtypeStruct((D, 6 * HD), jnp.bfloat16),
        grid=(4,),
        in_specs=[pl.BlockSpec((3, D // 4, HD), lambda i: (0, i, 0))] * 2,
        out_specs=pl.BlockSpec((D // 4, 6 * HD), lambda i: (i, 0)),
        compiler_params=params(12),
        cost_estimate=pl.CostEstimate(flops=0, bytes_accessed=4 * D * 6 * HD, transcendentals=0),
        name="pack",
    )(own, other)


def project_kernel(*refs):
    blocks, (weight_ref, gain_ref, q_ref, kv_ref) = refs[:4], refs[4:]
    x = jnp.concatenate([b[...] for b in blocks], axis=0)
    out = jnp.dot(x, weight_ref[...], preferred_element_type=jnp.float32)
    for head in range(2):
        at = head * 3 * HD
        q_ref[head] = normalized(out[:, at:at + HD]).astype(jnp.bfloat16)
        k = normalized(out[:, at + HD:at + 2 * HD]) * gain_ref[head:head + 1, :]
        kv_ref[head, 0] = k.astype(jnp.bfloat16)
        kv_ref[head, 1] = out[:, at + 2 * HD:at + 3 * HD].astype(jnp.bfloat16)


def project_call(blocks, weight, gain):
    return pl.pallas_call(
        project_kernel,
        out_shape=(
            jax.ShapeDtypeStruct((2, CHUNK, HD), jnp.bfloat16),
            jax.ShapeDtypeStruct((2, 2, CHUNK, HD), jnp.bfloat16),
        ),
        in_specs=[VMEM] * 6,
        out_specs=(VMEM, VMEM),
        compiler_params=params(12),
        cost_estimate=pl.CostEstimate(flops=2 * CHUNK * D * 768, bytes_accessed=2 * (D * 768 + CHUNK * D), transcendentals=0),
        name="project",
    )(*blocks, weight, gain)


def attend(q, k, v):
    logits = lax.dot_general(q, k, (((1,), (1,)), ((), ())), preferred_element_type=jnp.float32)
    exponent = jnp.exp2(logits * EXP2_SCALE).astype(jnp.bfloat16)
    wide = jnp.concatenate([v, jnp.ones_like(v)], axis=1)
    return jnp.dot(exponent, wide, preferred_element_type=jnp.float32)


def stale_kernel(tick, slots_ref, q_ref, own_k, own_v, other_k, other_v, *refs):
    fresh, total_ref = refs[:-1], refs[-1]
    for head, (k_ref, v_ref) in enumerate(((own_k, own_v), (other_k, other_v))):
        q = q_ref[head]
        total = jnp.zeros((CHUNK, 2 * HD), jnp.float32)
        for j in range(tick + 1, PATCHES):
            slot = slots_ref[j]
            total += attend(q, k_ref[slot], v_ref[slot])
        for ref in fresh:
            total += attend(q, ref[head, 0], ref[head, 1])
        total_ref[head] = total


def stale_call(tick, slots, q, caches, fresh):
    keys = TOKP * (PATCHES - 1)
    return pl.pallas_call(
        functools.partial(stale_kernel, tick),
        out_shape=jax.ShapeDtypeStruct((2, CHUNK, 2 * HD), jnp.float32),
        in_specs=[SMEM] + [VMEM] * (5 + len(fresh)),
        out_specs=VMEM,
        compiler_params=params(20),
        cost_estimate=pl.CostEstimate(flops=16 * CHUNK * keys * HD, bytes_accessed=8 * keys * HD, transcendentals=2 * CHUNK * keys),
        name="stale",
    )(slots, q, *caches, *fresh)


def attended_rows(q_ref, t_ref, kvs, out_ref):
    for head in range(2):
        total = t_ref[head]
        for mine, theirs in kvs:
            k = jnp.concatenate([mine[head, 0], theirs[1 - head, 0]], axis=0)
            v = jnp.concatenate([mine[head, 1], theirs[1 - head, 1]], axis=0)
            total += attend(q_ref[head], k, v)
        attended = (total[:, :HD] / total[:, HD:]).astype(jnp.bfloat16)
        out_ref[:, :, head * HD:(head + 1) * HD] = attended.reshape(4, ROWS, HD)


def across_kernel(q_ref, t_ref, kva, rxa, kvb, rxb, out_ref):
    attended_rows(q_ref, t_ref, ((kva, rxa), (kvb, rxb)), out_ref)


def along_kernel(place_ref, q_ref, t_ref, kva, rxa, kvb, rxb, out_ref, kv_ref):
    attended_rows(q_ref, t_ref, ((kva, rxa), (kvb, rxb)), out_ref)
    y_at, x_at, core = place_ref[0], place_ref[1], place_ref[2]
    for dy, (mine, theirs) in enumerate(((kva, rxa), (kvb, rxb))):
        for dx in range(4):
            chip = lax.rem(y_at + dy, 2) * 4 + lax.rem(x_at + dx, 4)
            rows = pl.ds(dx * ROWS, ROWS)
            here = pl.ds(pl.multiple_of((chip * 2 + core) * ROWS, ROWS), ROWS)
            there = pl.ds(pl.multiple_of((chip * 2 + 1 - core) * ROWS, ROWS), ROWS)
            for head in range(2):
                for part in range(2):
                    kv_ref[head, part, here, :] = mine[head, part, rows, :]
                    kv_ref[head, part, there, :] = theirs[1 - head, part, rows, :]


FRESH_COST = pl.CostEstimate(
    flops=16 * CHUNK * TOKP * HD, bytes_accessed=8 * TOKP * HD, transcendentals=2 * CHUNK * TOKP
)


def across_call(q, total, kvs, received):
    return pl.pallas_call(
        across_kernel,
        out_shape=jax.ShapeDtypeStruct((4, ROWS, 2 * HD), jnp.bfloat16),
        in_specs=[VMEM] * 6,
        out_specs=VMEM,
        compiler_params=params(12),
        cost_estimate=FRESH_COST,
        name="across",
    )(q, total, kvs[0], received[0], kvs[1], received[1])


def along_call(place, q, total, kvs, received):
    return pl.pallas_call(
        along_kernel,
        out_shape=(
            jax.ShapeDtypeStruct((4, ROWS, 2 * HD), jnp.bfloat16),
            jax.ShapeDtypeStruct((2, 2, TOKP, HD), jnp.bfloat16),
        ),
        in_specs=[SMEM] + [VMEM] * 6,
        out_specs=(VMEM, VMEM),
        compiler_params=params(12),
        cost_estimate=FRESH_COST,
        name="along",
    )(place, q, total, kvs[0], received[0], kvs[1], received[1])


def output_part(a_ref, w_ref, u_ref):
    a = jnp.concatenate([a_ref[dx] for dx in range(4)], axis=0)
    weight = jnp.concatenate([w_ref[...], u_ref[...]], axis=0)
    return jnp.dot(a, weight, preferred_element_type=jnp.float32)


OUTPUT_COST = pl.CostEstimate(
    flops=2 * 4 * ROWS * 2 * HD * D, bytes_accessed=2 * 2 * HD * D, transcendentals=0
)


def near_kernel(kept_ref, w_ref, u_ref, part_ref):
    part_ref[...] = output_part(kept_ref, w_ref, u_ref)


def near_call(kept, w, u):
    return pl.pallas_call(
        near_kernel,
        out_shape=jax.ShapeDtypeStruct((4 * ROWS, D), jnp.float32),
        in_specs=[VMEM] * 3,
        out_specs=VMEM,
        compiler_params=params(12),
        cost_estimate=OUTPUT_COST,
        name="near",
    )(kept, w, u)


def output_kernel(part_ref, got_ref, w_ref, u_ref, own_ref, p1_ref, p2_ref, p3_ref):
    total = part_ref[...] + output_part(got_ref, w_ref, u_ref)
    own_ref[...] = total[:ROWS]
    for dx, ref in ((1, p1_ref), (2, p2_ref), (3, p3_ref)):
        ref[...] = total[dx * ROWS:(dx + 1) * ROWS].astype(jnp.bfloat16)


def output_call(part, got, w, u):
    rows = jax.ShapeDtypeStruct((ROWS, D), jnp.bfloat16)
    return pl.pallas_call(
        output_kernel,
        out_shape=(jax.ShapeDtypeStruct((ROWS, D), jnp.float32), rows, rows, rows),
        in_specs=[VMEM] * 4,
        out_specs=(VMEM,) * 4,
        compiler_params=params(12),
        cost_estimate=OUTPUT_COST,
        name="output",
    )(part, got, w, u)


def finished(inflow_ref, own_ref, p1_ref, p2_ref, p3_ref, modulate_ref):
    attention = own_ref[...]
    for ref in (p1_ref, p2_ref, p3_ref):
        attention += ref[...].astype(jnp.float32)
    return (inflow_ref[...].astype(jnp.float32) + modulate_ref[2:3, :] * attention).astype(jnp.bfloat16)


def finish_kernel(*refs):
    refs[-1][...] = finished(*refs[:-1])


def finish_call(inflow, own, parts, modulate):
    return pl.pallas_call(
        finish_kernel,
        out_shape=jax.ShapeDtypeStruct((ROWS, D), jnp.bfloat16),
        in_specs=[VMEM] * 6,
        out_specs=VMEM,
        compiler_params=params(8),
        cost_estimate=pl.CostEstimate(flops=6 * ROWS * D, bytes_accessed=14 * ROWS * D, transcendentals=0),
        name="finish",
    )(inflow, own, *parts, modulate)


def last_kernel(*refs):
    out_ref, rows, stored = refs[-3:]
    rows[...] = finished(*refs[:6])
    copy = pltpu.make_async_copy(rows, out_ref.at[TICKS - 1], stored)
    copy.start()
    copy.wait()


def last_call(inflow, own, parts, modulate, whole):
    anywhere = pl.BlockSpec(memory_space=pl.ANY)
    return pl.pallas_call(
        last_kernel,
        out_shape=jax.ShapeDtypeStruct((TICKS, ROWS, D), jnp.bfloat16),
        in_specs=[VMEM] * 6 + [anywhere],
        out_specs=anywhere,
        scratch_shapes=[pltpu.VMEM((ROWS, D), jnp.bfloat16), pltpu.SemaphoreType.DMA],
        input_output_aliases={6: 0},
        compiler_params=params(8),
        cost_estimate=pl.CostEstimate(flops=6 * ROWS * D, bytes_accessed=14 * ROWS * D, transcendentals=0),
        name="last",
    )(inflow, own, *parts, modulate, whole)


def body(
    waiting,
    entering,
    patch_order,
    step_index,
    modulation,
    projection,
    key_gain,
    output_weight,
    stale_keys,
    stale_values,
):
    section = lax.axis_index("section")
    blk = lax.axis_index("blk")
    place = jnp.stack([blk // 8, (blk // 2) % 4, blk % 2]).astype(jnp.int32)
    modulate = lax.dynamic_index_in_dim(modulation[0], step_index[0], 0, keepdims=False)
    positions = jnp.mod(jnp.arange(PATCHES, dtype=jnp.int32) - section, PATCHES)
    slots = jnp.sum(jnp.where(positions[:, None] == jnp.arange(PATCHES)[None, :], patch_order[None, :], 0), axis=1)
    first = (section == 0).astype(jnp.int32).reshape(1)

    gain = jnp.concatenate([key_gain, shift(key_gain, 0, 0, 1)], axis=0)
    flat = projection[0].transpose(1, 0, 2)

    fresh = []
    produced_rows = []
    fresh_rows = []
    for tick in range(TICKS):
        if tick == 0:
            inflow, normed = norm_call(jnp.zeros((1,), jnp.int32), waiting[0], waiting[0], modulate)
        else:
            passed = passed_along(produced_rows[-1], "section", 1)
            inflow, normed = norm_call(first, entering[tick - 1], passed, modulate)
        xm = shift(normed, 0, 1, 0)
        xp = shift(normed, 0, -1, 0)
        y0 = shift(normed, 1, 0, 0)
        x2 = shift(normed, 0, 2, 0)
        ym = shift(y0, 0, 1, 0)
        yp = shift(y0, 0, -1, 0)
        if tick == 0:
            y2 = shift(y0, 0, 2, 0)
            first_step = (xm, xp, y0)
            flat_late, _ = lax.optimization_barrier((flat, first_step))
            weight = pack_call(flat, shift(flat_late, 0, 0, 1))
            own_keys, _ = lax.optimization_barrier((stale_keys[0], (x2, ym, yp, weight)))
            own_values, _ = lax.optimization_barrier((stale_values[0], (y2, weight)))
            caches = (own_keys, own_values, shift(own_keys, 0, 0, 1), shift(own_values, 0, 0, 1))
            out_own, _ = lax.optimization_barrier((output_weight[0], first_step))
            out_across = shift(out_own, 1, 0, 0)
            weights = (out_own, shift(out_own, 0, 0, 1), out_across)
        else:
            y2 = shift(x2, 1, 0, 0)
        queries, kvs, received, totals = [], [], [], []
        for blocks in ((normed, xp, x2, xm), (y0, yp, y2, ym)):
            if totals:
                blocks, totals[0] = lax.optimization_barrier((blocks, totals[0]))
            q, kv = project_call(blocks, weight, gain)
            queries.append(q)
            kvs.append(kv)
            received.append(shift(kv, 0, 0, 1))
            totals.append(stale_call(tick, slots, q, caches, fresh))
        sent = across_call(queries[1], totals[1], kvs, received)
        kept, kv_all = along_call(place, queries[0], totals[0], kvs, received)
        if tick == 0:
            out_across, _ = lax.optimization_barrier((out_across, sent))
            weights = weights + (shift(out_across, 0, 0, 1),)
        fresh.append(kv_all)
        fresh_rows.append(kv_all[0].transpose(1, 0, 2))
        part = near_call(kept, *weights[:2])
        own, p1, p2, p3 = output_call(part, shift(sent, 1, 0, 0), *weights[2:])
        parts = (shift(p2, 0, 2, 0), shift(p1, 0, 1, 0), shift(p3, 0, 3, 0))
        if tick < TICKS - 1:
            produced_rows.append(finish_call(inflow, own, parts, modulate))
        else:
            whole = jnp.stack(produced_rows + [jnp.zeros_like(inflow)])
            layer_out = last_call(inflow, own, parts, modulate, whole)
    return (layer_out[None], jnp.stack(fresh_rows)[None])


def solution(mesh):
    placed = (
        P("section", "blk", None),
        P(None, "blk", None),
        P(),
        P(),
        P("section", None, None, None),
        P("section", None, None, "blk"),
        P("section", "blk"),
        P("section", "blk", None),
        P("section", None, None, "blk"),
        P("section", None, None, "blk"),
    )
    return jax.shard_map(
        body,
        mesh=mesh,
        in_specs=placed,
        out_specs=(P("section", None, "blk", None), P("section", None, None, None, "blk")),
        check_vma=False,
    )
```

```python
import functools
import math

import jax
import jax.numpy as jnp
from jax import lax
from jax.experimental import pallas as pl
from jax.experimental.pallas import tpu as pltpu
from jax.sharding import PartitionSpec as P

D = 3072
HD = 128
PATCHES = 12
TICKS = 4
TOKP = 512
ROWS = 32
BLOCKS = 8
HALF = BLOCKS * ROWS
CHUNK = HALF // 2

epsilon = 1e-06
EXP2_SCALE = HD ** (-0.5) * math.log2(math.e)

VMEM = pl.BlockSpec(memory_space=pltpu.VMEM)
SMEM = pl.BlockSpec(memory_space=pltpu.SMEM)


def params(mib):
    return pltpu.CompilerParams(vmem_limit_bytes=mib * 1024 * 1024)


def shift(x, dy, dx, dc):
    pairs = []
    for y in range(2):
        for a in range(4):
            for c in range(2):
                target = (((y + dy) % 2) * 4 + (a + dx) % 4) * 2 + (c + dc) % 2
                pairs.append(((y * 4 + a) * 2 + c, target))
    return lax.ppermute(x, "blk", pairs)


def passed_along(x, axis, by):
    size = lax.axis_size(axis)
    pairs = [(i, i + by) for i in range(size) if 0 <= i + by < size]
    return lax.ppermute(x, axis, pairs)


def normalized(t):
    return t / jnp.sqrt(jnp.mean(t * t, axis=-1, keepdims=True) + epsilon)


def norm_kernel(first_ref, entering_ref, passed_ref, modulate_ref, inflow_ref, normed_ref):
    first = jnp.full((ROWS, D), first_ref[0], jnp.int32) == 1
    inflow = jnp.where(first, entering_ref[...].astype(jnp.float32), passed_ref[...].astype(jnp.float32))
    inflow_ref[...] = inflow.astype(jnp.bfloat16)
    normed = normalized(inflow) * (1.0 + modulate_ref[1:2, :]) + modulate_ref[0:1, :]
    normed_ref[...] = normed.astype(jnp.bfloat16)


def norm_call(first, entering, passed, modulate):
    shape = jax.ShapeDtypeStruct((ROWS, D), jnp.bfloat16)
    return pl.pallas_call(
        norm_kernel,
        out_shape=(shape, shape),
        in_specs=[SMEM, VMEM, VMEM, VMEM],
        out_specs=(VMEM, VMEM),
        compiler_params=params(8),
        cost_estimate=pl.CostEstimate(flops=10 * ROWS * D, bytes_accessed=10 * ROWS * D, transcendentals=0),
        name="norm",
    )(first, entering, passed, modulate)


def pack_kernel(own_ref, other_ref, out_ref):
    for part in range(3):
        out_ref[:, part * HD:(part + 1) * HD] = own_ref[part]
        out_ref[:, (3 + part) * HD:(4 + part) * HD] = other_ref[part]


def pack_call(own, other):
    return pl.pallas_call(
        pack_kernel,
        out_shape=jax.ShapeDtypeStruct((D, 6 * HD), jnp.bfloat16),
        grid=(4,),
        in_specs=[pl.BlockSpec((3, D // 4, HD), lambda i: (0, i, 0))] * 2,
        out_specs=pl.BlockSpec((D // 4, 6 * HD), lambda i: (i, 0)),
        compiler_params=params(12),
        cost_estimate=pl.CostEstimate(flops=0, bytes_accessed=4 * D * 6 * HD, transcendentals=0),
        name="pack",
    )(own, other)


def project_kernel(*refs):
    blocks, (weight_ref, gain_ref, q_ref, kv_ref) = refs[:4], refs[4:]
    x = jnp.concatenate([b[...] for b in blocks], axis=0)
    out = jnp.dot(x, weight_ref[...], preferred_element_type=jnp.float32)
    for head in range(2):
        at = head * 3 * HD
        q_ref[head] = normalized(out[:, at:at + HD]).astype(jnp.bfloat16)
        k = normalized(out[:, at + HD:at + 2 * HD]) * gain_ref[head:head + 1, :]
        kv_ref[head, 0] = k.astype(jnp.bfloat16)
        kv_ref[head, 1] = out[:, at + 2 * HD:at + 3 * HD].astype(jnp.bfloat16)


def project_call(blocks, weight, gain):
    return pl.pallas_call(
        project_kernel,
        out_shape=(
            jax.ShapeDtypeStruct((2, CHUNK, HD), jnp.bfloat16),
            jax.ShapeDtypeStruct((2, 2, CHUNK, HD), jnp.bfloat16),
        ),
        in_specs=[VMEM] * 6,
        out_specs=(VMEM, VMEM),
        compiler_params=params(12),
        cost_estimate=pl.CostEstimate(flops=2 * CHUNK * D * 768, bytes_accessed=2 * (D * 768 + CHUNK * D), transcendentals=0),
        name="project",
    )(*blocks, weight, gain)


def attend(q, k, v):
    logits = lax.dot_general(q, k, (((1,), (1,)), ((), ())), preferred_element_type=jnp.float32)
    exponent = jnp.exp2(logits * EXP2_SCALE).astype(jnp.bfloat16)
    wide = jnp.concatenate([v, jnp.ones_like(v)], axis=1)
    return jnp.dot(exponent, wide, preferred_element_type=jnp.float32)


def stale_kernel(tick, slots_ref, q_ref, own_k, own_v, other_k, other_v, *refs):
    fresh, total_ref = refs[:-1], refs[-1]
    for head, (k_ref, v_ref) in enumerate(((own_k, own_v), (other_k, other_v))):
        q = q_ref[head]
        total = jnp.zeros((CHUNK, 2 * HD), jnp.float32)
        for j in range(tick + 1, PATCHES):
            slot = slots_ref[j]
            total += attend(q, k_ref[slot], v_ref[slot])
        for ref in fresh:
            total += attend(q, ref[head, 0], ref[head, 1])
        total_ref[head] = total


def stale_call(tick, slots, q, caches, fresh):
    keys = TOKP * (PATCHES - 1)
    return pl.pallas_call(
        functools.partial(stale_kernel, tick),
        out_shape=jax.ShapeDtypeStruct((2, CHUNK, 2 * HD), jnp.float32),
        in_specs=[SMEM] + [VMEM] * (5 + len(fresh)),
        out_specs=VMEM,
        compiler_params=params(20),
        cost_estimate=pl.CostEstimate(flops=16 * CHUNK * keys * HD, bytes_accessed=8 * keys * HD, transcendentals=2 * CHUNK * keys),
        name="stale",
    )(slots, q, *caches, *fresh)


CHUNKS = (((0, 0), (0, 1), (1, 0), (3, 0)), ((2, 0), (1, 1), (3, 1), (2, 1)))


def fresh_kernel(place_ref, qa, qb, ta, tb, kva, rxa, kvb, rxb, kept_ref, sent_ref, kv_ref):
    y_at, x_at, core = place_ref[0], place_ref[1], place_ref[2]
    for index, (mine, theirs) in enumerate(((kva, rxa), (kvb, rxb))):
        for n, (dx, dy) in enumerate(CHUNKS[index]):
            chip = lax.rem(y_at + dy, 2) * 4 + lax.rem(x_at + dx, 4)
            rows = pl.ds(n * ROWS, ROWS)
            here = pl.ds(pl.multiple_of((chip * 2 + core) * ROWS, ROWS), ROWS)
            there = pl.ds(pl.multiple_of((chip * 2 + 1 - core) * ROWS, ROWS), ROWS)
            for head in range(2):
                for part in range(2):
                    kv_ref[head, part, here, :] = mine[head, part, rows, :]
                    kv_ref[head, part, there, :] = theirs[1 - head, part, rows, :]
    for head in range(2):
        q = jnp.concatenate([qa[head], qb[head]], axis=0)
        total = jnp.concatenate([ta[head], tb[head]], axis=0)
        for mine, theirs in ((kva, rxa), (kvb, rxb)):
            k = jnp.concatenate([mine[head, 0], theirs[1 - head, 0]], axis=0)
            v = jnp.concatenate([mine[head, 1], theirs[1 - head, 1]], axis=0)
            total += attend(q, k, v)
        attended = (total[:, :HD] / total[:, HD:]).astype(jnp.bfloat16)
        for n, (dx, dy) in enumerate(CHUNKS[0] + CHUNKS[1]):
            target = sent_ref if dy else kept_ref
            target[dx, :, head * HD:(head + 1) * HD] = attended[n * ROWS:(n + 1) * ROWS]


def fresh_call(place, queries, totals, kvs, received):
    rows = jax.ShapeDtypeStruct((4, ROWS, 2 * HD), jnp.bfloat16)
    return pl.pallas_call(
        fresh_kernel,
        out_shape=(rows, rows, jax.ShapeDtypeStruct((2, 2, TOKP, HD), jnp.bfloat16)),
        in_specs=[SMEM] + [VMEM] * 8,
        out_specs=(VMEM, VMEM, VMEM),
        compiler_params=params(12),
        cost_estimate=pl.CostEstimate(flops=16 * HALF * TOKP * HD, bytes_accessed=8 * TOKP * HD, transcendentals=2 * HALF * TOKP),
        name="fresh",
    )(place, *queries, *totals, kvs[0], received[0], kvs[1], received[1])


def output_kernel(kept_ref, got_ref, w0, w1, w2, w3, own_ref, p1_ref, p2_ref, p3_ref):
    total = None
    for a_ref, w, u in ((kept_ref, w0, w1), (got_ref, w2, w3)):
        a = jnp.concatenate([a_ref[dx] for dx in range(4)], axis=0)
        weight = jnp.concatenate([w[...], u[...]], axis=0)
        part = jnp.dot(a, weight, preferred_element_type=jnp.float32)
        total = part if total is None else total + part
    own_ref[...] = total[:ROWS]
    for dx, ref in ((1, p1_ref), (2, p2_ref), (3, p3_ref)):
        ref[...] = total[dx * ROWS:(dx + 1) * ROWS].astype(jnp.bfloat16)


def output_call(kept, got, weights):
    part = jax.ShapeDtypeStruct((ROWS, D), jnp.bfloat16)
    return pl.pallas_call(
        output_kernel,
        out_shape=(jax.ShapeDtypeStruct((ROWS, D), jnp.float32), part, part, part),
        in_specs=[VMEM] * 6,
        out_specs=(VMEM,) * 4,
        compiler_params=params(12),
        cost_estimate=pl.CostEstimate(flops=2 * 4 * ROWS * 4 * HD * D, bytes_accessed=2 * 4 * HD * D, transcendentals=0),
        name="output",
    )(kept, got, *weights)


def finished(inflow_ref, own_ref, p1_ref, p2_ref, p3_ref, modulate_ref):
    attention = own_ref[...]
    for ref in (p1_ref, p2_ref, p3_ref):
        attention += ref[...].astype(jnp.float32)
    return (inflow_ref[...].astype(jnp.float32) + modulate_ref[2:3, :] * attention).astype(jnp.bfloat16)


def finish_kernel(*refs):
    refs[-1][...] = finished(*refs[:-1])


def finish_call(inflow, own, parts, modulate):
    return pl.pallas_call(
        finish_kernel,
        out_shape=jax.ShapeDtypeStruct((ROWS, D), jnp.bfloat16),
        in_specs=[VMEM] * 6,
        out_specs=VMEM,
        compiler_params=params(8),
        cost_estimate=pl.CostEstimate(flops=6 * ROWS * D, bytes_accessed=14 * ROWS * D, transcendentals=0),
        name="finish",
    )(inflow, own, *parts, modulate)


def last_kernel(*refs):
    out_ref, rows, stored = refs[-3:]
    rows[...] = finished(*refs[:6])
    copy = pltpu.make_async_copy(rows, out_ref.at[TICKS - 1], stored)
    copy.start()
    copy.wait()


def last_call(inflow, own, parts, modulate, whole):
    anywhere = pl.BlockSpec(memory_space=pl.ANY)
    return pl.pallas_call(
        last_kernel,
        out_shape=jax.ShapeDtypeStruct((TICKS, ROWS, D), jnp.bfloat16),
        in_specs=[VMEM] * 6 + [anywhere],
        out_specs=anywhere,
        scratch_shapes=[pltpu.VMEM((ROWS, D), jnp.bfloat16), pltpu.SemaphoreType.DMA],
        input_output_aliases={6: 0},
        compiler_params=params(8),
        cost_estimate=pl.CostEstimate(flops=6 * ROWS * D, bytes_accessed=14 * ROWS * D, transcendentals=0),
        name="last",
    )(inflow, own, *parts, modulate, whole)


def body(
    waiting,
    entering,
    patch_order,
    step_index,
    modulation,
    projection,
    key_gain,
    output_weight,
    stale_keys,
    stale_values,
):
    section = lax.axis_index("section")
    blk = lax.axis_index("blk")
    place = jnp.stack([blk // 8, (blk // 2) % 4, blk % 2]).astype(jnp.int32)
    modulate = lax.dynamic_index_in_dim(modulation[0], step_index[0], 0, keepdims=False)
    positions = jnp.mod(jnp.arange(PATCHES, dtype=jnp.int32) - section, PATCHES)
    slots = jnp.sum(jnp.where(positions[:, None] == jnp.arange(PATCHES)[None, :], patch_order[None, :], 0), axis=1)
    first = (section == 0).astype(jnp.int32).reshape(1)

    gain_other = shift(key_gain, 0, 0, 1)
    gain = jnp.concatenate([key_gain, gain_other], axis=0)
    flat = projection[0].transpose(1, 0, 2)
    flat_late, _ = lax.optimization_barrier((flat, gain_other))
    flat_other = shift(flat_late, 0, 0, 1)

    fresh = []
    produced_rows = []
    fresh_rows = []
    for tick in range(TICKS):
        if tick == 0:
            inflow, normed = norm_call(jnp.zeros((1,), jnp.int32), waiting[0], waiting[0], modulate)
        else:
            passed = passed_along(produced_rows[-1], "section", 1)
            inflow, normed = norm_call(first, entering[tick - 1], passed, modulate)
        xm = shift(normed, 0, 1, 0)
        xp = shift(normed, 0, -1, 0)
        y0 = shift(normed, 1, 0, 0)
        x2 = shift(normed, 0, 2, 0)
        ym = shift(y0, 0, 1, 0)
        yp = shift(y0, 0, -1, 0)
        if tick == 0:
            y2 = shift(y0, 0, 2, 0)
            first_step = (xm, xp, y0, x2, flat_other)
            weight = pack_call(flat, flat_other)
            own_keys, _ = lax.optimization_barrier((stale_keys[0], first_step))
            own_values, _ = lax.optimization_barrier((stale_values[0], first_step))
            caches = (own_keys, own_values, shift(own_keys, 0, 0, 1), shift(own_values, 0, 0, 1))
            out_own, _ = lax.optimization_barrier((output_weight[0], (ym, yp)))
            out_across = shift(out_own, 1, 0, 0)
            weights = (out_own, shift(out_own, 0, 0, 1), out_across)
        else:
            y2 = shift(x2, 1, 0, 0)
        queries, kvs, received, totals = [], [], [], []
        for blocks in ((normed, y0, xp, xm), (x2, yp, ym, y2)):
            q, kv = project_call(blocks, weight, gain)
            queries.append(q)
            kvs.append(kv)
            received.append(shift(kv, 0, 0, 1))
            totals.append(stale_call(tick, slots, q, caches, fresh))
        kept, sent, kv_all = fresh_call(place, queries, totals, kvs, received)
        if tick == 0:
            out_across, _ = lax.optimization_barrier((out_across, kept))
            weights = weights + (shift(out_across, 0, 0, 1),)
        fresh.append(kv_all)
        fresh_rows.append(kv_all[0].transpose(1, 0, 2))
        own, p1, p2, p3 = output_call(kept, shift(sent, 1, 0, 0), weights)
        parts = (shift(p2, 0, 2, 0), shift(p1, 0, 1, 0), shift(p3, 0, 3, 0))
        if tick < TICKS - 1:
            produced_rows.append(finish_call(inflow, own, parts, modulate))
        else:
            whole = jnp.stack(produced_rows + [jnp.zeros_like(inflow)])
            layer_out = last_call(inflow, own, parts, modulate, whole)
    return (layer_out[None], jnp.stack(fresh_rows)[None])


def solution(mesh):
    placed = (
        P("section", "blk", None),
        P(None, "blk", None),
        P(),
        P(),
        P("section", None, None, None),
        P("section", None, None, "blk"),
        P("section", "blk"),
        P("section", "blk", None),
        P("section", None, None, "blk"),
        P("section", None, None, "blk"),
    )
    return jax.shard_map(
        body,
        mesh=mesh,
        in_specs=placed,
        out_specs=(P("section", None, "blk", None), P("section", None, None, None, "blk")),
        check_vma=False,
    )
```

```python
import functools
import math

import jax
import jax.numpy as jnp
from jax import lax
from jax.experimental import pallas as pl
from jax.experimental.pallas import tpu as pltpu
from jax.sharding import PartitionSpec as P

D = 3072
HD = 128
PATCHES = 12
TICKS = 4
TOKP = 512
ROWS = 32
BLOCKS = 8
HALF = BLOCKS * ROWS
CHUNK = HALF

epsilon = 1e-06
EXP2_SCALE = HD ** (-0.5) * math.log2(math.e)

VMEM = pl.BlockSpec(memory_space=pltpu.VMEM)
SMEM = pl.BlockSpec(memory_space=pltpu.SMEM)


def params(mib):
    return pltpu.CompilerParams(vmem_limit_bytes=mib * 1024 * 1024)


def shift(x, dy, dx, dc):
    pairs = []
    for y in range(2):
        for a in range(4):
            for c in range(2):
                target = (((y + dy) % 2) * 4 + (a + dx) % 4) * 2 + (c + dc) % 2
                pairs.append(((y * 4 + a) * 2 + c, target))
    return lax.ppermute(x, "blk", pairs)


def passed_along(x, axis, by):
    size = lax.axis_size(axis)
    pairs = [(i, i + by) for i in range(size) if 0 <= i + by < size]
    return lax.ppermute(x, axis, pairs)


def normalized(t):
    return t / jnp.sqrt(jnp.mean(t * t, axis=-1, keepdims=True) + epsilon)


def norm_kernel(first_ref, entering_ref, passed_ref, modulate_ref, inflow_ref, normed_ref):
    first = jnp.full((ROWS, D), first_ref[0], jnp.int32) == 1
    inflow = jnp.where(first, entering_ref[...].astype(jnp.float32), passed_ref[...].astype(jnp.float32))
    inflow_ref[...] = inflow.astype(jnp.bfloat16)
    normed = normalized(inflow) * (1.0 + modulate_ref[1:2, :]) + modulate_ref[0:1, :]
    normed_ref[...] = normed.astype(jnp.bfloat16)


def norm_call(first, entering, passed, modulate):
    shape = jax.ShapeDtypeStruct((ROWS, D), jnp.bfloat16)
    return pl.pallas_call(
        norm_kernel,
        out_shape=(shape, shape),
        in_specs=[SMEM, VMEM, VMEM, VMEM],
        out_specs=(VMEM, VMEM),
        compiler_params=params(8),
        cost_estimate=pl.CostEstimate(flops=10 * ROWS * D, bytes_accessed=10 * ROWS * D, transcendentals=0),
        name="norm",
    )(first, entering, passed, modulate)


def pack_kernel(own_ref, other_ref, out_ref):
    for part in range(3):
        out_ref[:, part * HD:(part + 1) * HD] = own_ref[part]
        out_ref[:, (3 + part) * HD:(4 + part) * HD] = other_ref[part]


def pack_call(own, other):
    return pl.pallas_call(
        pack_kernel,
        out_shape=jax.ShapeDtypeStruct((D, 6 * HD), jnp.bfloat16),
        grid=(4,),
        in_specs=[pl.BlockSpec((3, D // 4, HD), lambda i: (0, i, 0))] * 2,
        out_specs=pl.BlockSpec((D // 4, 6 * HD), lambda i: (i, 0)),
        compiler_params=params(12),
        cost_estimate=pl.CostEstimate(flops=0, bytes_accessed=4 * D * 6 * HD, transcendentals=0),
        name="pack",
    )(own, other)


def project_kernel(*refs):
    blocks, (weight_ref, gain_ref, q_ref, kv_ref) = refs[:BLOCKS], refs[BLOCKS:]
    x = jnp.concatenate([b[...] for b in blocks], axis=0)
    out = jnp.dot(x, weight_ref[...], preferred_element_type=jnp.float32)
    for head in range(2):
        at = head * 3 * HD
        q_ref[head] = normalized(out[:, at:at + HD]).astype(jnp.bfloat16)
        k = normalized(out[:, at + HD:at + 2 * HD]) * gain_ref[head:head + 1, :]
        kv_ref[head, 0] = k.astype(jnp.bfloat16)
        kv_ref[head, 1] = out[:, at + 2 * HD:at + 3 * HD].astype(jnp.bfloat16)


def project_call(blocks, weight, gain):
    return pl.pallas_call(
        project_kernel,
        out_shape=(
            jax.ShapeDtypeStruct((2, CHUNK, HD), jnp.bfloat16),
            jax.ShapeDtypeStruct((2, 2, CHUNK, HD), jnp.bfloat16),
        ),
        in_specs=[VMEM] * (BLOCKS + 2),
        out_specs=(VMEM, VMEM),
        compiler_params=params(16),
        cost_estimate=pl.CostEstimate(flops=2 * CHUNK * D * 768, bytes_accessed=2 * (D * 768 + CHUNK * D), transcendentals=0),
        name="project",
    )(*blocks, weight, gain)


def attend(q, k, v):
    logits = lax.dot_general(q, k, (((1,), (1,)), ((), ())), preferred_element_type=jnp.float32)
    exponent = jnp.exp2(logits * EXP2_SCALE).astype(jnp.bfloat16)
    wide = jnp.concatenate([v, jnp.ones_like(v)], axis=1)
    return jnp.dot(exponent, wide, preferred_element_type=jnp.float32)


def stale_kernel(tick, slots_ref, q_ref, own_k, own_v, other_k, other_v, *refs):
    fresh, total_ref = refs[:-1], refs[-1]
    for head, (k_ref, v_ref) in enumerate(((own_k, own_v), (other_k, other_v))):
        q = q_ref[head]
        total = jnp.zeros((CHUNK, 2 * HD), jnp.float32)
        for j in range(tick + 1, PATCHES):
            slot = slots_ref[j]
            total += attend(q, k_ref[slot], v_ref[slot])
        for ref in fresh:
            total += attend(q, ref[head, 0], ref[head, 1])
        total_ref[head] = total


def stale_call(tick, slots, q, caches, fresh):
    keys = TOKP * (PATCHES - 1)
    return pl.pallas_call(
        functools.partial(stale_kernel, tick),
        out_shape=jax.ShapeDtypeStruct((2, CHUNK, 2 * HD), jnp.float32),
        in_specs=[SMEM] + [VMEM] * (5 + len(fresh)),
        out_specs=VMEM,
        compiler_params=params(20),
        cost_estimate=pl.CostEstimate(flops=16 * CHUNK * keys * HD, bytes_accessed=8 * keys * HD, transcendentals=2 * CHUNK * keys),
        name="stale",
    )(slots, q, *caches, *fresh)


PLACES = ((0, 0), (0, 1), (1, 0), (3, 0), (2, 0), (1, 1), (3, 1), (2, 1))


def fresh_kernel(place_ref, q_ref, t_ref, mine, theirs, kept_ref, sent_ref, kv_ref):
    y_at, x_at, core = place_ref[0], place_ref[1], place_ref[2]
    for n, (dx, dy) in enumerate(PLACES):
        chip = lax.rem(y_at + dy, 2) * 4 + lax.rem(x_at + dx, 4)
        rows = pl.ds(n * ROWS, ROWS)
        here = pl.ds(pl.multiple_of((chip * 2 + core) * ROWS, ROWS), ROWS)
        there = pl.ds(pl.multiple_of((chip * 2 + 1 - core) * ROWS, ROWS), ROWS)
        for head in range(2):
            for part in range(2):
                kv_ref[head, part, here, :] = mine[head, part, rows, :]
                kv_ref[head, part, there, :] = theirs[1 - head, part, rows, :]
    for head in range(2):
        k = jnp.concatenate([mine[head, 0], theirs[1 - head, 0]], axis=0)
        v = jnp.concatenate([mine[head, 1], theirs[1 - head, 1]], axis=0)
        total = t_ref[head] + attend(q_ref[head], k, v)
        attended = (total[:, :HD] / total[:, HD:]).astype(jnp.bfloat16)
        for n, (dx, dy) in enumerate(PLACES):
            target = sent_ref if dy else kept_ref
            target[dx, :, head * HD:(head + 1) * HD] = attended[n * ROWS:(n + 1) * ROWS]


def fresh_call(place, q, total, kv, received):
    rows = jax.ShapeDtypeStruct((4, ROWS, 2 * HD), jnp.bfloat16)
    return pl.pallas_call(
        fresh_kernel,
        out_shape=(rows, rows, jax.ShapeDtypeStruct((2, 2, TOKP, HD), jnp.bfloat16)),
        in_specs=[SMEM] + [VMEM] * 4,
        out_specs=(VMEM, VMEM, VMEM),
        compiler_params=params(12),
        cost_estimate=pl.CostEstimate(flops=16 * HALF * TOKP * HD, bytes_accessed=8 * TOKP * HD, transcendentals=2 * HALF * TOKP),
        name="fresh",
    )(place, q, total, kv, received)


def output_kernel(kept_ref, got_ref, w0, w1, w2, w3, own_ref, p1_ref, p2_ref, p3_ref):
    total = None
    for a_ref, w, u in ((kept_ref, w0, w1), (got_ref, w2, w3)):
        a = jnp.concatenate([a_ref[dx] for dx in range(4)], axis=0)
        weight = jnp.concatenate([w[...], u[...]], axis=0)
        part = jnp.dot(a, weight, preferred_element_type=jnp.float32)
        total = part if total is None else total + part
    own_ref[...] = total[:ROWS]
    for dx, ref in ((1, p1_ref), (2, p2_ref), (3, p3_ref)):
        ref[...] = total[dx * ROWS:(dx + 1) * ROWS].astype(jnp.bfloat16)


def output_call(kept, got, weights):
    part = jax.ShapeDtypeStruct((ROWS, D), jnp.bfloat16)
    return pl.pallas_call(
        output_kernel,
        out_shape=(jax.ShapeDtypeStruct((ROWS, D), jnp.float32), part, part, part),
        in_specs=[VMEM] * 6,
        out_specs=(VMEM,) * 4,
        compiler_params=params(12),
        cost_estimate=pl.CostEstimate(flops=2 * 4 * ROWS * 4 * HD * D, bytes_accessed=2 * 4 * HD * D, transcendentals=0),
        name="output",
    )(kept, got, *weights)


def finished(inflow_ref, own_ref, p1_ref, p2_ref, p3_ref, modulate_ref):
    attention = own_ref[...]
    for ref in (p1_ref, p2_ref, p3_ref):
        attention += ref[...].astype(jnp.float32)
    return (inflow_ref[...].astype(jnp.float32) + modulate_ref[2:3, :] * attention).astype(jnp.bfloat16)


def finish_kernel(*refs):
    refs[-1][...] = finished(*refs[:-1])


def finish_call(inflow, own, parts, modulate):
    return pl.pallas_call(
        finish_kernel,
        out_shape=jax.ShapeDtypeStruct((ROWS, D), jnp.bfloat16),
        in_specs=[VMEM] * 6,
        out_specs=VMEM,
        compiler_params=params(8),
        cost_estimate=pl.CostEstimate(flops=6 * ROWS * D, bytes_accessed=14 * ROWS * D, transcendentals=0),
        name="finish",
    )(inflow, own, *parts, modulate)


def last_kernel(*refs):
    out_ref, rows, stored = refs[-3:]
    rows[...] = finished(*refs[:6])
    copy = pltpu.make_async_copy(rows, out_ref.at[TICKS - 1], stored)
    copy.start()
    copy.wait()


def last_call(inflow, own, parts, modulate, whole):
    anywhere = pl.BlockSpec(memory_space=pl.ANY)
    return pl.pallas_call(
        last_kernel,
        out_shape=jax.ShapeDtypeStruct((TICKS, ROWS, D), jnp.bfloat16),
        in_specs=[VMEM] * 6 + [anywhere],
        out_specs=anywhere,
        scratch_shapes=[pltpu.VMEM((ROWS, D), jnp.bfloat16), pltpu.SemaphoreType.DMA],
        input_output_aliases={6: 0},
        compiler_params=params(8),
        cost_estimate=pl.CostEstimate(flops=6 * ROWS * D, bytes_accessed=14 * ROWS * D, transcendentals=0),
        name="last",
    )(inflow, own, *parts, modulate, whole)


def body(
    waiting,
    entering,
    patch_order,
    step_index,
    modulation,
    projection,
    key_gain,
    output_weight,
    stale_keys,
    stale_values,
):
    section = lax.axis_index("section")
    blk = lax.axis_index("blk")
    place = jnp.stack([blk // 8, (blk // 2) % 4, blk % 2]).astype(jnp.int32)
    modulate = lax.dynamic_index_in_dim(modulation[0], step_index[0], 0, keepdims=False)
    positions = jnp.mod(jnp.arange(PATCHES, dtype=jnp.int32) - section, PATCHES)
    slots = jnp.sum(jnp.where(positions[:, None] == jnp.arange(PATCHES)[None, :], patch_order[None, :], 0), axis=1)
    first = (section == 0).astype(jnp.int32).reshape(1)

    gain_other = shift(key_gain, 0, 0, 1)
    gain = jnp.concatenate([key_gain, gain_other], axis=0)
    flat = projection[0].transpose(1, 0, 2)
    flat_late, _ = lax.optimization_barrier((flat, gain_other))
    flat_other = shift(flat_late, 0, 0, 1)

    fresh = []
    produced_rows = []
    fresh_rows = []
    for tick in range(TICKS):
        if tick == 0:
            inflow, normed = norm_call(jnp.zeros((1,), jnp.int32), waiting[0], waiting[0], modulate)
        else:
            passed = passed_along(produced_rows[-1], "section", 1)
            inflow, normed = norm_call(first, entering[tick - 1], passed, modulate)
        xm = shift(normed, 0, 1, 0)
        xp = shift(normed, 0, -1, 0)
        y0 = shift(normed, 1, 0, 0)
        x2 = shift(normed, 0, 2, 0)
        ym = shift(y0, 0, 1, 0)
        yp = shift(y0, 0, -1, 0)
        if tick == 0:
            y2 = shift(y0, 0, 2, 0)
            first_step = (xm, xp, y0, x2, flat_other)
            weight = pack_call(flat, flat_other)
            own_keys, _ = lax.optimization_barrier((stale_keys[0], first_step))
            own_values, _ = lax.optimization_barrier((stale_values[0], first_step))
            caches = (own_keys, own_values, shift(own_keys, 0, 0, 1), shift(own_values, 0, 0, 1))
            out_own, _ = lax.optimization_barrier((output_weight[0], (ym, yp)))
            out_across = shift(out_own, 1, 0, 0)
            weights = (out_own, shift(out_own, 0, 0, 1), out_across)
        else:
            y2 = shift(x2, 1, 0, 0)
        q, kv = project_call((normed, y0, xp, xm, x2, yp, ym, y2), weight, gain)
        received = shift(kv, 0, 0, 1)
        total = stale_call(tick, slots, q, caches, fresh)
        kept, sent, kv_all = fresh_call(place, q, total, kv, received)
        if tick == 0:
            out_across, _ = lax.optimization_barrier((out_across, kept))
            weights = weights + (shift(out_across, 0, 0, 1),)
        fresh.append(kv_all)
        fresh_rows.append(kv_all[0].transpose(1, 0, 2))
        own, p1, p2, p3 = output_call(kept, shift(sent, 1, 0, 0), weights)
        parts = (shift(p2, 0, 2, 0), shift(p1, 0, 1, 0), shift(p3, 0, 3, 0))
        if tick < TICKS - 1:
            produced_rows.append(finish_call(inflow, own, parts, modulate))
        else:
            whole = jnp.stack(produced_rows + [jnp.zeros_like(inflow)])
            layer_out = last_call(inflow, own, parts, modulate, whole)
    return (layer_out[None], jnp.stack(fresh_rows)[None])


def solution(mesh):
    placed = (
        P("section", "blk", None),
        P(None, "blk", None),
        P(),
        P(),
        P("section", None, None, None),
        P("section", None, None, "blk"),
        P("section", "blk"),
        P("section", "blk", None),
        P("section", None, None, "blk"),
        P("section", None, None, "blk"),
    )
    return jax.shard_map(
        body,
        mesh=mesh,
        in_specs=placed,
        out_specs=(P("section", None, "blk", None), P("section", None, None, None, "blk")),
        check_vma=False,
    )
```

```python
import functools
import math

import jax
import jax.numpy as jnp
from jax import lax
from jax.experimental import pallas as pl
from jax.experimental.pallas import tpu as pltpu
from jax.sharding import PartitionSpec as P

D = 3072
HD = 128
PATCHES = 12
TICKS = 4
TOKP = 512
ROWS = 32
BLOCKS = 8
HALF = BLOCKS * ROWS
CHUNK = HALF

epsilon = 1e-06
EXP2_SCALE = HD ** (-0.5) * math.log2(math.e)

VMEM = pl.BlockSpec(memory_space=pltpu.VMEM)
SMEM = pl.BlockSpec(memory_space=pltpu.SMEM)


def params(mib):
    return pltpu.CompilerParams(vmem_limit_bytes=mib * 1024 * 1024)


def shift(x, dy, dx, dc):
    pairs = []
    for y in range(2):
        for a in range(4):
            for c in range(2):
                target = (((y + dy) % 2) * 4 + (a + dx) % 4) * 2 + (c + dc) % 2
                pairs.append(((y * 4 + a) * 2 + c, target))
    return lax.ppermute(x, "blk", pairs)


def passed_along(x, axis, by):
    size = lax.axis_size(axis)
    pairs = [(i, i + by) for i in range(size) if 0 <= i + by < size]
    return lax.ppermute(x, axis, pairs)


def normalized(t):
    return t / jnp.sqrt(jnp.mean(t * t, axis=-1, keepdims=True) + epsilon)


def norm_kernel(first_ref, entering_ref, passed_ref, modulate_ref, inflow_ref, normed_ref):
    first = jnp.full((ROWS, D), first_ref[0], jnp.int32) == 1
    inflow = jnp.where(first, entering_ref[...].astype(jnp.float32), passed_ref[...].astype(jnp.float32))
    inflow_ref[...] = inflow.astype(jnp.bfloat16)
    normed = normalized(inflow) * (1.0 + modulate_ref[1:2, :]) + modulate_ref[0:1, :]
    normed_ref[...] = normed.astype(jnp.bfloat16)


def norm_call(first, entering, passed, modulate):
    shape = jax.ShapeDtypeStruct((ROWS, D), jnp.bfloat16)
    return pl.pallas_call(
        norm_kernel,
        out_shape=(shape, shape),
        in_specs=[SMEM, VMEM, VMEM, VMEM],
        out_specs=(VMEM, VMEM),
        compiler_params=params(8),
        cost_estimate=pl.CostEstimate(flops=10 * ROWS * D, bytes_accessed=10 * ROWS * D, transcendentals=0),
        name="norm",
    )(first, entering, passed, modulate)


def pack_kernel(own_ref, other_ref, out_ref):
    for part in range(3):
        out_ref[:, part * HD:(part + 1) * HD] = own_ref[part]
        out_ref[:, (3 + part) * HD:(4 + part) * HD] = other_ref[part]


def pack_call(own, other):
    return pl.pallas_call(
        pack_kernel,
        out_shape=jax.ShapeDtypeStruct((D, 6 * HD), jnp.bfloat16),
        grid=(4,),
        in_specs=[pl.BlockSpec((3, D // 4, HD), lambda i: (0, i, 0))] * 2,
        out_specs=pl.BlockSpec((D // 4, 6 * HD), lambda i: (i, 0)),
        compiler_params=params(12),
        cost_estimate=pl.CostEstimate(flops=0, bytes_accessed=4 * D * 6 * HD, transcendentals=0),
        name="pack",
    )(own, other)


def project_kernel(*refs):
    blocks, (weight_ref, gain_ref, q_ref, kv_ref) = refs[:BLOCKS], refs[BLOCKS:]
    x = jnp.concatenate([b[...] for b in blocks], axis=0)
    out = jnp.dot(x, weight_ref[...], preferred_element_type=jnp.float32)
    for head in range(2):
        at = head * 3 * HD
        q_ref[head] = normalized(out[:, at:at + HD]).astype(jnp.bfloat16)
        k = normalized(out[:, at + HD:at + 2 * HD]) * gain_ref[head:head + 1, :]
        kv_ref[head, 0] = k.astype(jnp.bfloat16)
        kv_ref[head, 1] = out[:, at + 2 * HD:at + 3 * HD].astype(jnp.bfloat16)


def project_call(blocks, weight, gain):
    return pl.pallas_call(
        project_kernel,
        out_shape=(
            jax.ShapeDtypeStruct((2, CHUNK, HD), jnp.bfloat16),
            jax.ShapeDtypeStruct((2, 2, CHUNK, HD), jnp.bfloat16),
        ),
        in_specs=[VMEM] * (BLOCKS + 2),
        out_specs=(VMEM, VMEM),
        compiler_params=params(16),
        cost_estimate=pl.CostEstimate(flops=2 * CHUNK * D * 768, bytes_accessed=2 * (D * 768 + CHUNK * D), transcendentals=0),
        name="project",
    )(*blocks, weight, gain)


def attend(q, k, v):
    logits = lax.dot_general(q, k, (((1,), (1,)), ((), ())), preferred_element_type=jnp.float32)
    exponent = jnp.exp2(logits * EXP2_SCALE).astype(jnp.bfloat16)
    wide = jnp.concatenate([v, jnp.ones_like(v)], axis=1)
    return jnp.dot(exponent, wide, preferred_element_type=jnp.float32)


def stale_kernel(tick, slots_ref, q_ref, own_k, own_v, other_k, other_v, *refs):
    fresh, total_ref = refs[:-1], refs[-1]
    for head, (k_ref, v_ref) in enumerate(((own_k, own_v), (other_k, other_v))):
        q = q_ref[head]
        total = jnp.zeros((CHUNK, 2 * HD), jnp.float32)
        for j in range(tick + 1, PATCHES):
            slot = slots_ref[j]
            total += attend(q, k_ref[slot], v_ref[slot])
        for ref in fresh:
            total += attend(q, ref[head, 0], ref[head, 1])
        total_ref[head] = total


def stale_call(tick, slots, q, caches, fresh):
    keys = TOKP * (PATCHES - 1)
    return pl.pallas_call(
        functools.partial(stale_kernel, tick),
        out_shape=jax.ShapeDtypeStruct((2, CHUNK, 2 * HD), jnp.float32),
        in_specs=[SMEM] + [VMEM] * (5 + len(fresh)),
        out_specs=VMEM,
        compiler_params=params(20),
        cost_estimate=pl.CostEstimate(flops=16 * CHUNK * keys * HD, bytes_accessed=8 * keys * HD, transcendentals=2 * CHUNK * keys),
        name="stale",
    )(slots, q, *caches, *fresh)


PLACES = ((0, 0), (0, 1), (1, 0), (3, 0), (2, 0), (1, 1), (3, 1), (2, 1))


def fresh_kernel(place_ref, q_ref, t_ref, mine, theirs, kept_ref, sent_ref, kv_ref):
    y_at, x_at, core = place_ref[0], place_ref[1], place_ref[2]
    for n, (dx, dy) in enumerate(PLACES):
        chip = lax.rem(y_at + dy, 2) * 4 + lax.rem(x_at + dx, 4)
        rows = pl.ds(n * ROWS, ROWS)
        here = pl.ds(pl.multiple_of((chip * 2 + core) * ROWS, ROWS), ROWS)
        there = pl.ds(pl.multiple_of((chip * 2 + 1 - core) * ROWS, ROWS), ROWS)
        for head in range(2):
            for part in range(2):
                kv_ref[head, part, here, :] = mine[head, part, rows, :]
                kv_ref[head, part, there, :] = theirs[1 - head, part, rows, :]
    for head in range(2):
        k = jnp.concatenate([mine[head, 0], theirs[1 - head, 0]], axis=0)
        v = jnp.concatenate([mine[head, 1], theirs[1 - head, 1]], axis=0)
        total = t_ref[head] + attend(q_ref[head], k, v)
        attended = (total[:, :HD] / total[:, HD:]).astype(jnp.bfloat16)
        for n, (dx, dy) in enumerate(PLACES):
            target = sent_ref if dy else kept_ref
            target[dx, :, head * HD:(head + 1) * HD] = attended[n * ROWS:(n + 1) * ROWS]


def fresh_call(place, q, total, kv, received):
    rows = jax.ShapeDtypeStruct((4, ROWS, 2 * HD), jnp.bfloat16)
    return pl.pallas_call(
        fresh_kernel,
        out_shape=(rows, rows, jax.ShapeDtypeStruct((2, 2, TOKP, HD), jnp.bfloat16)),
        in_specs=[SMEM] + [VMEM] * 4,
        out_specs=(VMEM, VMEM, VMEM),
        compiler_params=params(12),
        cost_estimate=pl.CostEstimate(flops=16 * HALF * TOKP * HD, bytes_accessed=8 * TOKP * HD, transcendentals=2 * HALF * TOKP),
        name="fresh",
    )(place, q, total, kv, received)


def output_kernel(kept_ref, got_ref, w0, w1, w2, w3, own_ref, p1_ref, p2_ref, p3_ref):
    total = None
    for a_ref, w, u in ((kept_ref, w0, w1), (got_ref, w2, w3)):
        a = jnp.concatenate([a_ref[dx] for dx in range(4)], axis=0)
        weight = jnp.concatenate([w[...], u[...]], axis=0)
        part = jnp.dot(a, weight, preferred_element_type=jnp.float32)
        total = part if total is None else total + part
    own_ref[...] = total[:ROWS]
    for dx, ref in ((1, p1_ref), (2, p2_ref), (3, p3_ref)):
        ref[...] = total[dx * ROWS:(dx + 1) * ROWS].astype(jnp.bfloat16)


def output_call(kept, got, weights):
    part = jax.ShapeDtypeStruct((ROWS, D), jnp.bfloat16)
    return pl.pallas_call(
        output_kernel,
        out_shape=(jax.ShapeDtypeStruct((ROWS, D), jnp.float32), part, part, part),
        in_specs=[VMEM] * 6,
        out_specs=(VMEM,) * 4,
        compiler_params=params(12),
        cost_estimate=pl.CostEstimate(flops=2 * 4 * ROWS * 4 * HD * D, bytes_accessed=2 * 4 * HD * D, transcendentals=0),
        name="output",
    )(kept, got, *weights)


def finished(inflow_ref, own_ref, p1_ref, p2_ref, p3_ref, modulate_ref):
    attention = own_ref[...]
    for ref in (p1_ref, p2_ref, p3_ref):
        attention += ref[...].astype(jnp.float32)
    return (inflow_ref[...].astype(jnp.float32) + modulate_ref[2:3, :] * attention).astype(jnp.bfloat16)


def finish_kernel(*refs):
    refs[-1][...] = finished(*refs[:-1])


def finish_call(inflow, own, parts, modulate):
    return pl.pallas_call(
        finish_kernel,
        out_shape=jax.ShapeDtypeStruct((ROWS, D), jnp.bfloat16),
        in_specs=[VMEM] * 6,
        out_specs=VMEM,
        compiler_params=params(8),
        cost_estimate=pl.CostEstimate(flops=6 * ROWS * D, bytes_accessed=14 * ROWS * D, transcendentals=0),
        name="finish",
    )(inflow, own, *parts, modulate)


def last_kernel(*refs):
    out_ref, rows, stored = refs[-3:]
    rows[...] = finished(*refs[:6])
    copy = pltpu.make_async_copy(rows, out_ref.at[TICKS - 1], stored)
    copy.start()
    copy.wait()


def last_call(inflow, own, parts, modulate, whole):
    anywhere = pl.BlockSpec(memory_space=pl.ANY)
    return pl.pallas_call(
        last_kernel,
        out_shape=jax.ShapeDtypeStruct((TICKS, ROWS, D), jnp.bfloat16),
        in_specs=[VMEM] * 6 + [anywhere],
        out_specs=anywhere,
        scratch_shapes=[pltpu.VMEM((ROWS, D), jnp.bfloat16), pltpu.SemaphoreType.DMA],
        input_output_aliases={6: 0},
        compiler_params=params(8),
        cost_estimate=pl.CostEstimate(flops=6 * ROWS * D, bytes_accessed=14 * ROWS * D, transcendentals=0),
        name="last",
    )(inflow, own, *parts, modulate, whole)


def body(
    waiting,
    entering,
    patch_order,
    step_index,
    modulation,
    projection,
    key_gain,
    output_weight,
    stale_keys,
    stale_values,
):
    section = lax.axis_index("section")
    blk = lax.axis_index("blk")
    place = jnp.stack([blk // 8, (blk // 2) % 4, blk % 2]).astype(jnp.int32)
    modulate = lax.dynamic_index_in_dim(modulation[0], step_index[0], 0, keepdims=False)
    positions = jnp.mod(jnp.arange(PATCHES, dtype=jnp.int32) - section, PATCHES)
    slots = jnp.sum(jnp.where(positions[:, None] == jnp.arange(PATCHES)[None, :], patch_order[None, :], 0), axis=1)
    first = (section == 0).astype(jnp.int32).reshape(1)

    gain_other = shift(key_gain, 0, 0, 1)
    gain = jnp.concatenate([key_gain, gain_other], axis=0)
    flat = projection[0].transpose(1, 0, 2)
    flat_late, _ = lax.optimization_barrier((flat, gain_other))
    flat_other = shift(flat_late, 0, 0, 1)

    fresh = []
    produced_rows = []
    fresh_rows = []
    for tick in range(TICKS):
        if tick == 0:
            inflow, normed = norm_call(jnp.zeros((1,), jnp.int32), waiting[0], waiting[0], modulate)
        else:
            passed = passed_along(produced_rows[-1], "section", 1)
            inflow, normed = norm_call(first, entering[tick - 1], passed, modulate)
        xm = shift(normed, 0, 1, 0)
        xp = shift(normed, 0, -1, 0)
        y0 = shift(normed, 1, 0, 0)
        x2 = shift(normed, 0, 2, 0)
        ym = shift(y0, 0, 1, 0)
        yp = shift(y0, 0, -1, 0)
        if tick == 0:
            y2 = shift(y0, 0, 2, 0)
            first_step = (xm, xp, y0, x2, flat_other)
            weight = pack_call(flat, flat_other)
            own_keys, _ = lax.optimization_barrier((stale_keys[0], first_step))
            own_values, _ = lax.optimization_barrier((stale_values[0], first_step))
            caches = (own_keys, own_values, shift(own_keys, 0, 0, 1), shift(own_values, 0, 0, 1))
            out_own, _ = lax.optimization_barrier((output_weight[0], (ym, yp, weight)))
            out_across = shift(out_own, 1, 0, 0)
            weights = (out_own, shift(out_own, 0, 0, 1), out_across)
        else:
            y2 = shift(x2, 1, 0, 0)
        q, kv = project_call((normed, y0, xp, xm, x2, yp, ym, y2), weight, gain)
        received = shift(kv, 0, 0, 1)
        total = stale_call(tick, slots, q, caches, fresh)
        kept, sent, kv_all = fresh_call(place, q, total, kv, received)
        if tick == 0:
            out_across, _ = lax.optimization_barrier((out_across, kept))
            weights = weights + (shift(out_across, 0, 0, 1),)
        fresh.append(kv_all)
        fresh_rows.append(kv_all[0].transpose(1, 0, 2))
        own, p1, p2, p3 = output_call(kept, shift(sent, 1, 0, 0), weights)
        parts = (shift(p2, 0, 2, 0), shift(p1, 0, 1, 0), shift(p3, 0, 3, 0))
        if tick < TICKS - 1:
            produced_rows.append(finish_call(inflow, own, parts, modulate))
        else:
            whole = jnp.stack(produced_rows + [jnp.zeros_like(inflow)])
            layer_out = last_call(inflow, own, parts, modulate, whole)
    return (layer_out[None], jnp.stack(fresh_rows)[None])


def solution(mesh):
    placed = (
        P("section", "blk", None),
        P(None, "blk", None),
        P(),
        P(),
        P("section", None, None, None),
        P("section", None, None, "blk"),
        P("section", "blk"),
        P("section", "blk", None),
        P("section", None, None, "blk"),
        P("section", None, None, "blk"),
    )
    return jax.shard_map(
        body,
        mesh=mesh,
        in_specs=placed,
        out_specs=(P("section", None, "blk", None), P("section", None, None, None, "blk")),
        check_vma=False,
    )
```
